128 devices in a mesh: ctx: 16 (over z, y_lo, core), tp: 8 (over y_hi, x).
Axes of the slice: x: 4, y: 4 (y_hi: 2, y_lo: 2; y = y_hi * 2 + y_lo), z: 4, core: 2. Of those that a mesh axis runs over, the one named last changes fastest.
Arguments:
- query_in: bfloat16 [4096, 8192], P('ctx', 'tp'), may hold values from -6 to 6
- key_in: bfloat16 [4096, 8192], P('ctx', 'tp'), may hold values from -6 to 6
- value_in: bfloat16 [4096, 8192], P('ctx', 'tp'), may hold values from -6 to 6
- short_filter: float32 [3, 7, 8192], P(None, None, 'tp'), may hold values from -2 to 2
- long_filter: bfloat16 [128, 512], P(None, 'tp'), may hold values from -0.5 to 0.5
- skip_gain: float32 [8192], P('tp'), may hold values from 0.5 to 1.5
- out_weight: bfloat16 [8192, 8192], P('tp'), may hold values from -0.09375 to 0.09375
- grad_output: bfloat16 [4096, 8192], P('ctx', 'tp'), may hold values from -6 to 6
Outputs:
- output: bfloat16 [4096, 8192], P('ctx', 'tp')
- grad_query: bfloat16 [4096, 8192], P('ctx', 'tp')
- grad_key: bfloat16 [4096, 8192], P('ctx', 'tp')
- grad_value: bfloat16 [4096, 8192], P('ctx', 'tp')
- weight_grad: bfloat16 [8192, 8192], P('tp', 'ctx')
The draws below stay inside these ranges and needn't reach their ends.
All inputs are finite; a program needn't handle non-finite values.
Results may differ from the reference program's by a relative error of at most 0.023.
Values may be sent and summed in bfloat16 or wider, within the bound.
No kernel may reach another device: no remote copies, remote signals or barrier semaphores. Data moves between devices by JAX's collectives and lax.ppermute only.
A program may use at most 192 MiB of HBM per device.

```python
import jax
import jax.numpy as jnp
from jax import lax

D = 8192
TAPS = 128
SHORT = 7
GROUP = 16
TOK_DEV = 256
TOKENS = 4096
GROUPS = 512
N_CTX = 16


def spiked(values, key, source, target, shards_of, factor):
    def block_of(position):
        return (jnp.arange(values.shape[position]) // (values.shape[position] // shards_of)).reshape((-1,) + (1,) * (values.ndim - 1 - position))

    near = jax.random.permutation(key, shards_of)[block_of(target)]
    far = (block_of(target) + shards_of // 2) % shards_of
    return jnp.where((block_of(source) == near) | (block_of(source) == far), factor * values, values)


def levels(own_key, extent, cuts, smallest, high):
    loudness = 1.0
    for dim, parts in cuts:
        heights = jax.random.uniform(jax.random.fold_in(jax.random.fold_in(own_key, 6), dim), (parts,), jnp.float32, smallest / len(cuts), high / len(cuts))
        loudness = loudness * jnp.repeat(jnp.exp(heights), extent[dim] // parts).reshape((-1,) + (1,) * (len(extent) - 1 - dim))
    return loudness


def normal_values(rng, dims, width, most, split=(), kind=jnp.bfloat16):
    loudness = levels(rng, dims, split, -0.22, 0.18) if split else 1.0
    array = jax.random.normal(rng, dims, jnp.float32) * width * loudness
    return jnp.minimum(jnp.maximum(array, -most), most).astype(kind)


def gaussian_with(key, shape, spread, most, pieces, heavy, kind=jnp.bfloat16):
    drawn = spread * jax.random.normal(key, shape, jnp.float32)
    if pieces:
        drawn = drawn * levels(key, shape, pieces, -0.22, 0.18)
    return jnp.clip(spiked(drawn, jax.random.fold_in(key, 3), *heavy), -most, most).astype(kind)


def setup_inputs(seed: int = 0) -> dict:
    splits = jax.random.split(jax.random.key(seed), 9)
    query_in = normal_values(splits[0], (TOKENS, D), 1.0, 6.0, ((0, 16), (1, 8)))
    key_in = normal_values(splits[1], (TOKENS, D), 1.0, 6.0, ((0, 16), (1, 8)))
    value_in = normal_values(splits[2], (TOKENS, D), 1.0, 6.0, ((0, 16), (1, 8)))
    short_filter = normal_values(splits[3], (3, SHORT, D), SHORT ** -0.5, 2.0, ((2, 8),), jnp.float32)
    long_filter = normal_values(splits[4], (TAPS, GROUPS), TAPS ** -0.5, 0.5, ((1, 8),))
    skip_gain = jnp.clip(0.5 + 1.0 * jax.random.uniform(splits[5], (D,), jnp.float32) ** levels(splits[5], (D,), ((0, 8),), -0.2, 0.2), 0.5, 1.5)
    out_weight = gaussian_with(splits[6], (D, D), D ** -0.5, 0.09375, ((0, 8),), (0, 1, 8, 2.0))
    grad_output = gaussian_with(splits[7], (TOKENS, D), 1.0, 6.0, ((0, 16), (1, 8)), (0, 1, 16, 2.0))
    return dict(query_in=query_in, key_in=key_in, value_in=value_in, short_filter=short_filter, long_filter=long_filter, skip_gain=skip_gain, out_weight=out_weight, grad_output=grad_output)


def short_forward(signal, coeffs):
    rows_all = signal.shape[0]
    padded = jnp.pad(signal.astype(jnp.float32), ((SHORT - 1, 0), (0, 0)))
    running = jnp.zeros(signal.shape, jnp.float32)
    for offset in range(SHORT):
        first_row = SHORT - 1 - offset
        running = running + coeffs[offset] * padded[first_row:first_row + rows_all]
    return running


def short_backward(upstream, coeffs):
    rows_all = upstream.shape[0]
    padded = jnp.pad(upstream, ((0, SHORT - 1), (0, 0)))
    running = jnp.zeros(upstream.shape, jnp.float32)
    for offset in range(SHORT):
        running = running + coeffs[offset] * padded[offset:offset + rows_all]
    return running


def causal_long(signal, kernel):
    length = 2 * signal.shape[0]
    spectrum = jnp.fft.rfft(signal, n=length, axis=0) * jnp.fft.rfft(kernel, n=length, axis=0)
    return jnp.fft.irfft(spectrum, n=length, axis=0)[: signal.shape[0]]


def reference(query_in, key_in, value_in, short_filter, long_filter, skip_gain, out_weight, grad_output):
    kernel = jnp.repeat(long_filter.astype(jnp.float32), GROUP, axis=1)
    query_conv = short_forward(query_in, short_filter[0])
    key_conv = short_forward(key_in, short_filter[1])
    value_conv = short_forward(value_in, short_filter[2])
    kv_product = (key_conv * value_conv).astype(jnp.bfloat16)
    kv_wide = kv_product.astype(jnp.float32)
    carried = causal_long(kv_wide, kernel) + skip_gain * kv_wide
    query_gated = (query_conv * carried).astype(jnp.bfloat16)
    output = jnp.dot(query_gated, out_weight, preferred_element_type=jnp.float32).astype(jnp.bfloat16)
    grad_gated = jnp.dot(grad_output, out_weight.T, preferred_element_type=jnp.float32)
    grad_carried = (grad_gated * query_conv).astype(jnp.bfloat16)
    grad_query_conv = grad_gated * carried
    carried_wide = grad_carried.astype(jnp.float32)
    grad_products = jnp.flip(causal_long(jnp.flip(carried_wide, 0), kernel), 0) + skip_gain * carried_wide
    grad_key_conv = grad_products * value_conv
    grad_value_conv = grad_products * key_conv
    grad_query = short_backward(grad_query_conv, short_filter[0]).astype(jnp.bfloat16)
    grad_key = short_backward(grad_key_conv, short_filter[1]).astype(jnp.bfloat16)
    grad_value = short_backward(grad_value_conv, short_filter[2]).astype(jnp.bfloat16)
    grad_scale = float(TOKENS) ** -0.5

    def add_block(running, block_index):
        first_row = (block_index * TOK_DEV).astype(jnp.int32)
        gated_rows = lax.dynamic_slice_in_dim(query_gated, first_row, TOK_DEV, 0)
        cotangent_rows = lax.dynamic_slice_in_dim(grad_output, first_row, TOK_DEV, 0)
        partial_value = jnp.dot(gated_rows.T, cotangent_rows, preferred_element_type=jnp.float32) * grad_scale
        rounded = lax.optimization_barrier(partial_value.astype(jnp.bfloat16))
        return running + rounded.astype(jnp.float32), None

    summed, _ = lax.scan(add_block, jnp.zeros((D, D), jnp.float32), jnp.arange(N_CTX, dtype=jnp.int32))
    weight_grad = summed.astype(jnp.bfloat16)
    return (output, grad_query, grad_key, grad_value, weight_grad)
```

```python
import functools

import jax
import jax.numpy as jnp
from jax import lax
from jax.experimental import pallas as pl
from jax.experimental.pallas import tpu as pltpu
from jax.sharding import PartitionSpec as P

Z, YL, CORE, YH, X = 4, 2, 2, 2, 4
F32, BF16 = jnp.float32, jnp.bfloat16
HALO = 144
HEAD = 16
LANES = 128
VMEM_LIMIT = 48 * 1024 * 1024


def ctx_pairs(move):
    pairs = []
    for i in range(Z * YL * CORE):
        z, yl, c = move(i // 4, (i // 2) % 2, i % 2)
        pairs.append((i, (z % Z) * 4 + (yl % YL) * 2 + c % CORE))
    return pairs


def tp_pairs(move):
    pairs = []
    for j in range(YH * X):
        yh, x = move(j // 4, j % 4)
        pairs.append((j, (yh % YH) * 4 + x % X))
    return pairs


def along_x(a, d):
    return lax.ppermute(a, "tp", tp_pairs(lambda yh, x: (yh, x + d)))


def across_yh(a):
    return lax.ppermute(a, "tp", tp_pairs(lambda yh, x: (yh + 1, x)))


def along_z(a, d):
    return lax.ppermute(a, "ctx", ctx_pairs(lambda z, yl, c: (z + d, yl, c)))


def across_core(a):
    return lax.ppermute(a, "ctx", ctx_pairs(lambda z, yl, c: (z, yl, c + 1)))


def next_shard(a, d):
    n = Z * YL * CORE
    return lax.ppermute(a, "ctx", [(i, i + d) for i in range(n) if 0 <= i + d < n])


def to_owner_yl(a, phase):
    pairs = []
    for i in range(Z * YL * CORE):
        for j in range(YH * X):
            parity = (j % X + 1 + phase) % 2
            if (i // 2) % 2 != parity:
                pairs.append((i * YH * X + j, (i ^ 2) * YH * X + j))
    return lax.ppermute(a, ("ctx", "tp"), pairs)


def toeplitz_into(table, rows):
    for g in range(8):
        wide = jnp.broadcast_to(rows[g : g + 1, :], (LANES, 2 * LANES))
        table[g * LANES : (g + 1) * LANES, :] = pltpu.roll(
            wide, 0, 1, stride=1, stride_axis=0
        ).astype(BF16)


def pick_groups(res, rows):
    lane_group = (lax.broadcasted_iota(jnp.int32, (rows, res.shape[1]), 1) % LANES) // 16
    out = res[:rows]
    for g in range(1, 8):
        out = jnp.where(lane_group == g, res[g * rows : (g + 1) * rows], out)
    return out


def forward_kernel(q, k, v, hq, hk, hv, sf, taps, gain, qc_o, ca_o, kc_o, vc_o, qg_o, qgt_o, qs, ks, vs, table):
    n = q.shape[0]
    qs[:HEAD] = hq[...].astype(F32)
    qs[HEAD:] = q[...].astype(F32)
    ks[:HALO] = hk[...].astype(F32)
    ks[HALO:] = k[...].astype(F32)
    vs[:HALO] = hv[...].astype(F32)
    vs[HALO:] = v[...].astype(F32)
    toeplitz_into(table, taps[...])

    def short(scr, member, first, rows):
        acc = sf[member, 0:1, :] * scr[pl.ds(first, rows), :]
        for s in range(1, 7):
            acc = acc + sf[member, s : s + 1, :] * scr[pl.ds(first - s, rows), :]
        return acc

    qc = short(qs, 0, HEAD, n)
    kc = short(ks, 1, HALO - LANES, n + LANES)
    vc = short(vs, 2, HALO - LANES, n + LANES)
    kv = (kc * vc).astype(BF16)
    window = jnp.concatenate([kv[: 2 * LANES], kv[LANES:]], axis=1)
    res = pick_groups(jnp.dot(table[...], window, preferred_element_type=F32), LANES)
    carried = jnp.concatenate([res[:, :LANES], res[:, LANES:]], axis=0)
    carried = carried + gain[...] * kv[LANES:].astype(F32)
    qc_o[...] = qc
    ca_o[...] = carried
    kc_o[...] = kc[LANES:]
    vc_o[...] = vc[LANES:]
    gated = qc * carried
    qg_o[...] = gated.astype(BF16)
    qgt_o[...] = gated.T.astype(BF16)


def forward(q, k, v, hq, hk, hv, sf, taps, gain):
    n, ch = q.shape
    col = lambda rows: pl.BlockSpec((rows, LANES), lambda i: (0, i))
    return pl.pallas_call(
        forward_kernel,
        grid=(ch // LANES,),
        in_specs=[
            col(n), col(n), col(n), col(HEAD), col(HALO), col(HALO),
            pl.BlockSpec((3, 7, LANES), lambda i: (0, 0, i)),
            pl.BlockSpec((8, 2 * LANES), lambda i: (i, 0)),
            col(1),
        ],
        out_specs=[col(n)] * 5 + [pl.BlockSpec((LANES, n), lambda i: (i, 0))],
        out_shape=[jax.ShapeDtypeStruct((n, ch), F32)] * 4
        + [jax.ShapeDtypeStruct((n, ch), BF16), jax.ShapeDtypeStruct((ch, n), BF16)],
        scratch_shapes=[
            pltpu.VMEM((HEAD + n, LANES), F32),
            pltpu.VMEM((HALO + n, LANES), F32),
            pltpu.VMEM((HALO + n, LANES), F32),
            pltpu.VMEM((8 * LANES, 2 * LANES), BF16),
        ],
        compiler_params=pltpu.CompilerParams(vmem_limit_bytes=VMEM_LIMIT),
        cost_estimate=pl.CostEstimate(flops=10**9 * 4, bytes_accessed=8 * 2**20, transcendentals=0),
        name="forward",
    )(q, k, v, hq, hk, hv, sf, taps, gain)


def backward_kernel(gc, gq, vc, kc, hgc, hgq, hvc, hkc, sf, taps, gain, dq_o, dk_o, dv_o, gs, qs, ks, vs, table):
    n = gc.shape[0]
    gs[:n] = gc[...]
    gs[n : n + HALO] = hgc[...]
    gs[n + HALO :] = jnp.zeros((gs.shape[0] - n - HALO, LANES), BF16)
    toeplitz_into(table, taps[...])
    window = jnp.concatenate([gs[: 2 * LANES], gs[LANES : 3 * LANES]], axis=1)
    res = pick_groups(jnp.dot(table[...], window, preferred_element_type=F32), LANES)
    small = jnp.concatenate([table[g * LANES : g * LANES + HEAD] for g in range(8)], axis=0)
    tail = pick_groups(jnp.dot(small, gs[2 * LANES :], preferred_element_type=F32), HEAD)
    gp = jnp.concatenate([res[:, :LANES], res[:, LANES:]], axis=0) + gain[...] * gs[:n].astype(F32)
    gp_tail = tail + gain[...] * gs[n : n + HEAD].astype(F32)
    qs[:n] = gq[...]
    qs[n:] = hgq[...].astype(F32)
    ks[:n] = gp * vc[...]
    ks[n:] = gp_tail * hvc[...].astype(F32)
    vs[:n] = gp * kc[...]
    vs[n:] = gp_tail * hkc[...].astype(F32)

    def short(scr, member):
        acc = sf[member, 0:1, :] * scr[pl.ds(0, n), :]
        for s in range(1, 7):
            acc = acc + sf[member, s : s + 1, :] * scr[pl.ds(s, n), :]
        return acc.astype(BF16)

    dq_o[...] = short(qs, 0)
    dk_o[...] = short(ks, 1)
    dv_o[...] = short(vs, 2)


def backward(gc, gq, vc, kc, hgc, hgq, hvc, hkc, sf, taps, gain):
    n, ch = gc.shape
    col = lambda rows: pl.BlockSpec((rows, LANES), lambda i: (0, i))
    return pl.pallas_call(
        backward_kernel,
        grid=(ch // LANES,),
        in_specs=[
            col(n), col(n), col(n), col(n), col(HALO), col(HEAD), col(HEAD), col(HEAD),
            pl.BlockSpec((3, 7, LANES), lambda i: (0, 0, i)),
            pl.BlockSpec((8, 2 * LANES), lambda i: (i, 0)),
            col(1),
        ],
        out_specs=[col(n)] * 3,
        out_shape=[jax.ShapeDtypeStruct((n, ch), BF16)] * 3,
        scratch_shapes=[
            pltpu.VMEM((4 * LANES, LANES), BF16),
            pltpu.VMEM((n + HEAD, LANES), F32),
            pltpu.VMEM((n + HEAD, LANES), F32),
            pltpu.VMEM((n + HEAD, LANES), F32),
            pltpu.VMEM((8 * LANES, 2 * LANES), BF16),
        ],
        compiler_params=pltpu.CompilerParams(vmem_limit_bytes=VMEM_LIMIT),
        cost_estimate=pl.CostEstimate(flops=10**9 * 4, bytes_accessed=6 * 2**20, transcendentals=0),
        name="backward",
    )(gc, gq, vc, kc, hgc, hgq, hvc, hkc, sf, taps, gain)


def grad_kernel(with_start, cols, blocks, w, *refs):
    start, out, acc = refs if with_start else (None,) + refs
    i = pl.program_id(0)
    part = lax.dot_general(blocks[0], w[...], (((1,), (1,)), ((), ())), preferred_element_type=F32)

    @pl.when(i == 0)
    def _():
        acc[...] = part + start[...] if with_start else part

    @pl.when(i > 0)
    def _():
        acc[...] += part

    @pl.when(i == pl.num_programs(0) - 1)
    def _():
        out[...] = acc[...]


def grad_product(cols, blocks, w, start=None):
    n, rows, width = blocks.shape
    ch = w.shape[0]
    whole = pl.BlockSpec((rows, ch), lambda i, s: (0, 0))
    extra = [] if start is None else [start]
    return pl.pallas_call(
        functools.partial(grad_kernel, start is not None),
        grid_spec=pltpu.PrefetchScalarGridSpec(
            num_scalar_prefetch=1,
            grid=(n,),
            in_specs=[
                pl.BlockSpec((1, rows, width), lambda i, s: (i, 0, 0)),
                pl.BlockSpec((ch, width), lambda i, s: (0, s[i])),
            ]
            + [whole] * len(extra),
            out_specs=whole,
            scratch_shapes=[pltpu.VMEM((rows, ch), F32)],
        ),
        out_shape=jax.ShapeDtypeStruct((rows, ch), F32),
        compiler_params=pltpu.CompilerParams(vmem_limit_bytes=VMEM_LIMIT),
        cost_estimate=pl.CostEstimate(
            flops=2 * n * rows * width * ch, bytes_accessed=2 * n * width * ch, transcendentals=0
        ),
        name="grad_product",
    )(cols, blocks, w, *extra)


def project_kernel(n_add, tops, cols, qg, w, *refs):
    adds, out = refs[:n_add], refs[n_add]
    part = jnp.dot(qg[...], w[...], preferred_element_type=F32)
    if n_add == 2:
        part = part + adds[0][0].astype(F32) + adds[1][0].astype(F32)
    if n_add != 1:
        out[0] = part.astype(BF16)
    else:
        half = part.shape[0] // 2
        i = pl.program_id(0)

        @pl.when(i < tops)
        def _():
            out[0, :half] = (part[:half] + adds[0][0].astype(F32)).astype(BF16)
            out[0, half:] = part[half:].astype(BF16)

        @pl.when(i >= tops)
        def _():
            out[0, :half] = part[:half].astype(BF16)
            out[0, half:] = (part[half:] + adds[0][0].astype(F32)).astype(BF16)


def project(cols, qg, w, adds=()):
    n = cols.shape[0]
    rows, ch = qg.shape
    add_spec = [pl.BlockSpec((1,) + a.shape[1:], lambda i, s: (i, 0, 0)) for a in adds]
    return pl.pallas_call(
        functools.partial(project_kernel, len(adds), n // 2),
        grid_spec=pltpu.PrefetchScalarGridSpec(
            num_scalar_prefetch=1,
            grid=(n,),
            in_specs=[
                pl.BlockSpec((rows, ch), lambda i, s: (0, 0)),
                pl.BlockSpec((ch, ch), lambda i, s: (0, s[i])),
            ]
            + add_spec,
            out_specs=pl.BlockSpec((1, rows, ch), lambda i, s: (i, 0, 0)),
        ),
        out_shape=jax.ShapeDtypeStruct((n, rows, ch), BF16),
        compiler_params=pltpu.CompilerParams(vmem_limit_bytes=VMEM_LIMIT),
        cost_estimate=pl.CostEstimate(
            flops=2 * n * rows * ch * ch, bytes_accessed=2 * n * ch * ch, transcendentals=0
        ),
        name="project",
    )(cols, qg, w, *adds)


def on_device(query_in, key_in, value_in, short_filter, long_filter, skip_gain, out_weight, grad_output):
    n, ch = query_in.shape
    half = ch // 2
    ctx, tp = lax.axis_index("ctx"), lax.axis_index("tp")
    z, yl, c = ctx // 4, (ctx // 2) % 2, ctx % 2
    yh, x = tp // 4, tp % 4
    gain = skip_gain.reshape(1, ch)

    keep = lax.dynamic_slice_in_dim(grad_output, c * half, half, 1)
    give = lax.dynamic_slice_in_dim(grad_output, (1 - c) * half, half, 1)
    own = jnp.stack([keep, across_core(give)])
    r1, l1 = along_x(own, 1), along_x(own, -1)
    other = across_yh(own)
    halo = next_shard(
        jnp.concatenate([query_in[n - HEAD :], key_in[n - HALO :], value_in[n - HALO :]], axis=0), 1
    )
    r2, l2 = along_x(other, 1), along_x(other, -1)
    r3 = along_x(jnp.stack([r1[0], r2[0]]), 1)
    l3 = along_x(jnp.stack([l1[1], l2[1]]), -1)

    taps = long_filter.astype(F32).T
    none = jnp.zeros((taps.shape[0], 1), F32)
    pad = jnp.zeros((taps.shape[0], taps.shape[1] - 1), F32)
    taps_fwd = jnp.concatenate([none, taps[:, ::-1], pad], axis=1)
    taps_bwd = jnp.concatenate([taps, none, pad], axis=1)
    query_conv, carried, key_conv, value_conv, gated, gated_t = forward(
        query_in, key_in, value_in,
        halo[:HEAD], halo[HEAD : HEAD + HALO], halo[HEAD + HALO :],
        short_filter, taps_fwd, gain,
    )

    zr, zl = along_z(gated_t, 1), along_z(gated_t, -1)
    zfar = jnp.concatenate([along_z(zr[: ch // 2], 1), along_z(zl[ch // 2 :], -1)], axis=0)
    mine = jnp.concatenate([gated_t, zr, zl, zfar], axis=1)
    theirs = across_core(mine)

    near = jnp.stack([r1, l1, r2, l2])
    far = jnp.stack([own, jnp.stack([r3[0], l3[0]]), other, jnp.stack([r3[1], l3[1]])])

    def block_cols(dys, dxs, parts):
        dy, dx = jnp.array(dys), jnp.array(dxs)
        return (((yh + dy) % YH) * X + (x + dx) % X).astype(jnp.int32) * parts

    near_cols = block_cols([0, 0, 1, 1], [3, 1, 3, 1], 2) + c
    far_cols = block_cols([0, 0, 1, 1], [0, 2, 0, 2], 2) + c
    w = out_weight
    partial_gg = grad_product(near_cols, near.reshape(4, 2 * n, half), w)
    partial_gg = grad_product(far_cols, far.reshape(4, 2 * n, half), w, partial_gg)

    def for_plane(blocks, d, phase):
        plane = (z + d) % Z
        to_x = 2 * (plane % 2) + (x + 1 + phase) % 2
        dy = (plane // 2 + yh) % 2
        dx = (to_x - x) % X
        place = dy * 2 + (dx == 1 + phase).astype(jnp.int32)
        return lax.dynamic_index_in_dim(blocks, place, 0, keepdims=False)

    def weight_part(blocks, phase):
        got = [for_plane(blocks, 0, phase)] + [
            along_z(for_plane(blocks, d, phase), d) for d in (1, -1, 2)
        ]
        return got

    def weight_sum(got):
        rows_own = jnp.concatenate([g[0] for g in got], axis=0)
        rows_their = jnp.concatenate([g[1] for g in got], axis=0)
        total = jnp.dot(mine, rows_own, preferred_element_type=F32)
        total = total + jnp.dot(theirs, rows_their, preferred_element_type=F32)
        return (total * float(n * Z * YL * CORE) ** -0.5).astype(BF16)

    near_got = weight_part(near, 0)
    far_got = weight_part(far, 1)
    sum_a = weight_sum(near_got)
    recv_a = to_owner_yl(sum_a, 0)

    p2 = project(block_cols([0, 1], [2, 2], 1), gated, w)
    h = n // 2
    got_r = along_x(p2[:, :h], 1)
    got_l = along_x(p2[:, h:], -1)
    p1 = project(
        block_cols([0, 1, 0, 1], [1, 1, 3, 3], 1), gated, w, (jnp.concatenate([got_r, got_l], axis=0),)
    )
    from_r = along_x(p1[:2], 1)
    from_l = along_x(p1[2:], -1)
    p0 = project(block_cols([0, 1], [0, 0], 1), gated, w, (from_r, from_l))
    output = (p0[0].astype(F32) + across_yh(p0[1]).astype(F32)).astype(BF16)

    grad_gated = partial_gg[:n] + across_core(partial_gg[n:].astype(BF16)).astype(F32)
    grad_carried = (grad_gated * query_conv).astype(BF16)
    grad_query_conv = grad_gated * carried
    rim = next_shard(
        jnp.concatenate(
            [
                grad_carried[:HALO],
                grad_query_conv[:HEAD].astype(BF16),
                value_conv[:HEAD].astype(BF16),
                key_conv[:HEAD].astype(BF16),
            ],
            axis=0,
        ),
        -1,
    )
    a, b, d = HALO, HALO + HEAD, HALO + 2 * HEAD
    grad_query, grad_key, grad_value = backward(
        grad_carried, grad_query_conv, value_conv, key_conv,
        rim[:a], rim[a:b], rim[b:d], rim[d:],
        short_filter, taps_bwd, gain,
    )

    sum_b = weight_sum(far_got)
    recv_b = to_owner_yl(sum_b, 1)
    here = jnp.where(yl == (x + 1) % 2, sum_a, sum_b).astype(F32)
    weight_grad = (here + recv_a.astype(F32) + recv_b.astype(F32)).astype(BF16)
    return output, grad_query, grad_key, grad_value, weight_grad


def solution(mesh):
    return jax.shard_map(
        on_device,
        mesh=mesh,
        in_specs=(
            P("ctx", "tp"),
            P("ctx", "tp"),
            P("ctx", "tp"),
            P(None, None, "tp"),
            P(None, "tp"),
            P("tp"),
            P("tp", None),
            P("ctx", "tp"),
        ),
        out_specs=(P("ctx", "tp"), P("ctx", "tp"), P("ctx", "tp"), P("ctx", "tp"), P("tp", "ctx")),
        check_vma=False,
    )
```

```python
import functools

import jax
import jax.numpy as jnp
from jax import lax
from jax.experimental import pallas as pl
from jax.experimental.pallas import tpu as pltpu
from jax.sharding import PartitionSpec as P

Z, YL, CORE, YH, X = 4, 2, 2, 2, 4
F32, BF16 = jnp.float32, jnp.bfloat16
HALO = 144
HEAD = 16
LANES = 128
VMEM_LIMIT = 16 * 1024 * 1024
VMEM_MOST = 50 * 1024 * 1024


def cost(us):
    return pl.CostEstimate(flops=int(us * 4.6e9), bytes_accessed=2**16, transcendentals=0)


def ctx_pairs(move):
    pairs = []
    for i in range(Z * YL * CORE):
        z, yl, c = move(i // 4, (i // 2) % 2, i % 2)
        pairs.append((i, (z % Z) * 4 + (yl % YL) * 2 + c % CORE))
    return pairs


def tp_pairs(move):
    pairs = []
    for j in range(YH * X):
        yh, x = move(j // 4, j % 4)
        pairs.append((j, (yh % YH) * 4 + x % X))
    return pairs


def along_x(a, d):
    return lax.ppermute(a, "tp", tp_pairs(lambda yh, x: (yh, x + d)))


def across_yh(a):
    return lax.ppermute(a, "tp", tp_pairs(lambda yh, x: (yh + 1, x)))


def along_z(a, d):
    return lax.ppermute(a, "ctx", ctx_pairs(lambda z, yl, c: (z + d, yl, c)))


def across_core(a):
    return lax.ppermute(a, "ctx", ctx_pairs(lambda z, yl, c: (z, yl, c + 1)))


def next_shard(a, d):
    n = Z * YL * CORE
    return lax.ppermute(a, "ctx", [(i, i + d) for i in range(n) if 0 <= i + d < n])


def across_yl(a):
    return lax.ppermute(a, "ctx", ctx_pairs(lambda z, yl, c: (z, yl + 1, c)))


def any_specs(n):
    return [pl.BlockSpec(memory_space=pl.ANY)] * n


def toeplitz_into(table, rows):
    for g in range(8):
        wide = jnp.broadcast_to(rows[g : g + 1, :], (LANES, 2 * LANES))
        table[g * LANES : (g + 1) * LANES, :] = pltpu.roll(
            wide, 0, 1, stride=1, stride_axis=0
        ).astype(BF16)


def pick_groups(res, rows):
    lane_group = (lax.broadcasted_iota(jnp.int32, (rows, res.shape[1]), 1) % LANES) // 16
    out = res[:rows]
    for g in range(1, 8):
        out = jnp.where(lane_group == g, res[g * rows : (g + 1) * rows], out)
    return out


def forward_kernel(
    q, k, v, halo, sf, taps, gain, *refs
):
    qc_o, ca_o, kc_o, vc_o, qg_o, qgt_o, qs, ks, vs, table = refs[-10:]
    n = q.shape[0]
    qs[:HEAD] = halo[:HEAD].astype(F32)
    qs[HEAD:] = q[...].astype(F32)
    ks[:HALO] = halo[HEAD : HEAD + HALO].astype(F32)
    ks[HALO:] = k[...].astype(F32)
    vs[:HALO] = halo[HEAD + HALO :].astype(F32)
    vs[HALO:] = v[...].astype(F32)
    toeplitz_into(table, taps[...])

    def short(scr, member, first, rows):
        acc = sf[member, 0:1, :] * scr[pl.ds(first, rows), :]
        for s in range(1, 7):
            acc = acc + sf[member, s : s + 1, :] * scr[pl.ds(first - s, rows), :]
        return acc

    qc = short(qs, 0, HEAD, n)
    kc = short(ks, 1, HALO - LANES, n + LANES)
    vc = short(vs, 2, HALO - LANES, n + LANES)
    kv = (kc * vc).astype(BF16)
    window = jnp.concatenate([kv[: 2 * LANES], kv[LANES:]], axis=1)
    res = pick_groups(jnp.dot(table[...], window, preferred_element_type=F32), LANES)
    carried = jnp.concatenate([res[:, :LANES], res[:, LANES:]], axis=0)
    carried = carried + gain[...] * kv[LANES:].astype(F32)
    qc_o[...] = qc
    ca_o[...] = carried
    kc_o[...] = kc[LANES:]
    vc_o[...] = vc[LANES:]
    gated = qc * carried
    qg_o[...] = gated.astype(BF16)
    qgt_o[...] = gated.T.astype(BF16)


def forward(q, k, v, halo, sf, taps, gain, after):
    n, ch = q.shape
    col = lambda rows: pl.BlockSpec((rows, LANES), lambda i: (0, i))
    return pl.pallas_call(
        forward_kernel,
        grid=(ch // LANES,),
        in_specs=[
            col(n), col(n), col(n), col(HEAD + 2 * HALO),
            pl.BlockSpec((3, 7, LANES), lambda i: (0, 0, i)),
            pl.BlockSpec((8, 2 * LANES), lambda i: (i, 0)),
            col(1),
        ]
        + [pl.BlockSpec(memory_space=pl.ANY)] * len(after),
        out_specs=[col(n)] * 5 + [pl.BlockSpec((LANES, n), lambda i: (i, 0))],
        out_shape=[jax.ShapeDtypeStruct((n, ch), F32)] * 4
        + [jax.ShapeDtypeStruct((n, ch), BF16), jax.ShapeDtypeStruct((ch, n), BF16)],
        scratch_shapes=[
            pltpu.VMEM((HEAD + n, LANES), F32),
            pltpu.VMEM((HALO + n, LANES), F32),
            pltpu.VMEM((HALO + n, LANES), F32),
            pltpu.VMEM((8 * LANES, 2 * LANES), BF16),
        ],
        compiler_params=pltpu.CompilerParams(vmem_limit_bytes=VMEM_LIMIT),
        cost_estimate=cost(8),
        name="forward",
    )(q, k, v, halo, sf, taps, gain, *after)


def backward_kernel(gc, gq, vc, kc, rim, sf, taps, gain, *refs):
    dq_o, dk_o, dv_o, gs, qs, ks, vs, table = refs[-8:]
    n = gc.shape[0]
    gs[:n] = gc[...]
    gs[n : n + HALO] = rim[:HALO]
    gs[n + HALO :] = jnp.zeros((gs.shape[0] - n - HALO, LANES), BF16)
    toeplitz_into(table, taps[...])
    window = jnp.concatenate([gs[: 2 * LANES], gs[LANES : 3 * LANES]], axis=1)
    res = pick_groups(jnp.dot(table[...], window, preferred_element_type=F32), LANES)
    small = jnp.concatenate([table[g * LANES : g * LANES + HEAD] for g in range(8)], axis=0)
    tail = pick_groups(jnp.dot(small, gs[2 * LANES :], preferred_element_type=F32), HEAD)
    gp = jnp.concatenate([res[:, :LANES], res[:, LANES:]], axis=0) + gain[...] * gs[:n].astype(F32)
    gp_tail = tail + gain[...] * gs[n : n + HEAD].astype(F32)
    qs[:n] = gq[...]
    qs[n:] = rim[HALO + 0 * HEAD : HALO + 1 * HEAD].astype(F32)
    ks[:n] = gp * vc[...]
    ks[n:] = gp_tail * rim[HALO + 1 * HEAD : HALO + 2 * HEAD].astype(F32)
    vs[:n] = gp * kc[...]
    vs[n:] = gp_tail * rim[HALO + 2 * HEAD : HALO + 3 * HEAD].astype(F32)

    def short(scr, member):
        acc = sf[member, 0:1, :] * scr[pl.ds(0, n), :]
        for s in range(1, 7):
            acc = acc + sf[member, s : s + 1, :] * scr[pl.ds(s, n), :]
        return acc.astype(BF16)

    dq_o[...] = short(qs, 0)
    dk_o[...] = short(ks, 1)
    dv_o[...] = short(vs, 2)


def backward(gc, gq, vc, kc, rim, sf, taps, gain, after):
    n, ch = gc.shape
    col = lambda rows: pl.BlockSpec((rows, LANES), lambda i: (0, i))
    return pl.pallas_call(
        backward_kernel,
        grid=(ch // LANES,),
        in_specs=[
            col(n), col(n), col(n), col(n), col(HALO + 3 * HEAD),
            pl.BlockSpec((3, 7, LANES), lambda i: (0, 0, i)),
            pl.BlockSpec((8, 2 * LANES), lambda i: (i, 0)),
            col(1),
        ]
        + any_specs(len(after)),
        out_specs=[col(n)] * 3,
        out_shape=[jax.ShapeDtypeStruct((n, ch), BF16)] * 3,
        scratch_shapes=[
            pltpu.VMEM((4 * LANES, LANES), BF16),
            pltpu.VMEM((n + HEAD, LANES), F32),
            pltpu.VMEM((n + HEAD, LANES), F32),
            pltpu.VMEM((n + HEAD, LANES), F32),
            pltpu.VMEM((8 * LANES, 2 * LANES), BF16),
        ],
        compiler_params=pltpu.CompilerParams(vmem_limit_bytes=VMEM_LIMIT),
        cost_estimate=cost(8),
        name="backward",
    )(gc, gq, vc, kc, rim, sf, taps, gain, *after)


def grad_kernel(n_blocks, last, cols, *refs):
    blocks, w = refs[:n_blocks], refs[n_blocks]
    acc = refs[-1]
    i = pl.program_id(0)
    for k in range(n_blocks):

        @pl.when(i == k)
        def _():
            part = lax.dot_general(
                blocks[k][...], w[...], (((1,), (1,)), ((), ())), preferred_element_type=F32
            )
            if k == 0 and last:
                acc[...] = part + refs[n_blocks + 1][...]
            elif k == 0:
                acc[...] = part
            else:
                acc[...] += part

    if not last:

        @pl.when(i == n_blocks - 1)
        def _():
            refs[-2][...] = acc[...]

        return

    query_conv, carried, value_conv, key_conv = refs[n_blocks + 2 : n_blocks + 6]
    gc_o, gq_o, rim_o = refs[-4:-1]

    @pl.when(i == n_blocks - 1)
    def _():
        grad_carried = (acc[...] * query_conv[...]).astype(BF16)
        gc_o[...] = grad_carried
        gq = acc[...] * carried[...]
        gq_o[...] = gq
        rim_o[:HALO] = grad_carried[:HALO]
        for k, rows in enumerate((gq, value_conv, key_conv)):
            rim_o[HALO + k * HEAD : HALO + (k + 1) * HEAD] = rows[:HEAD].astype(BF16)


def grad_product(cols, blocks, w, rest=(), after=(), us=6.4):
    n = len(blocks)
    rows, width = blocks[0].shape
    ch = w.shape[0]
    whole = lambda r: pl.BlockSpec((r, ch), lambda i, s: (0, 0))
    if rest:
        outs = [
            jax.ShapeDtypeStruct((rows, ch), BF16),
            jax.ShapeDtypeStruct((rows, ch), F32),
            jax.ShapeDtypeStruct((HALO + 3 * HEAD, ch), BF16),
        ]
        rest_specs = [whole(rows)] * 3 + [whole(HEAD)] * 2
    else:
        outs, rest_specs = [jax.ShapeDtypeStruct((rows, ch), F32)], []
    return pl.pallas_call(
        functools.partial(grad_kernel, n, bool(rest)),
        grid_spec=pltpu.PrefetchScalarGridSpec(
            num_scalar_prefetch=1,
            grid=(n,),
            in_specs=[whole(rows)] * n
            + [pl.BlockSpec((ch, width), lambda i, s: (0, s[i]))]
            + rest_specs
            + any_specs(len(after)),
            out_specs=[whole(o.shape[0]) for o in outs],
            scratch_shapes=[pltpu.VMEM((rows, ch), F32)],
        ),
        out_shape=outs,
        compiler_params=pltpu.CompilerParams(vmem_limit_bytes=VMEM_MOST),
        cost_estimate=cost(us),
        name="grad_product",
    )(cols, *blocks, w, *rest, *after)


def project_kernel(n, cols, qg, w, *refs):
    i = pl.program_id(0)
    part = jnp.dot(qg[...], w[...], preferred_element_type=F32)
    for k in range(n):

        @pl.when(i == k)
        def _():
            refs[k - n][...] = part.astype(refs[k - n].dtype)


def project(cols, qg, w, kinds, after=(), us=3.2):
    n = len(kinds)
    rows, ch = qg.shape
    whole = pl.BlockSpec((rows, ch), lambda i, s: (0, 0))
    return pl.pallas_call(
        functools.partial(project_kernel, n),
        grid_spec=pltpu.PrefetchScalarGridSpec(
            num_scalar_prefetch=1,
            grid=(n,),
            in_specs=[whole, pl.BlockSpec((ch, ch), lambda i, s: (0, s[i]))] + any_specs(len(after)),
            out_specs=[whole] * n,
        ),
        out_shape=[jax.ShapeDtypeStruct((rows, ch), kind) for kind in kinds],
        compiler_params=pltpu.CompilerParams(vmem_limit_bytes=VMEM_MOST),
        cost_estimate=cost(us),
        name="project",
    )(cols, qg, w, *after)


def select_kernel(first, width, places, *refs):
    blocks, outs, sems = refs[:8], refs[-5:-1], refs[-1]
    core = places[8]
    for o in range(4):
        for t in range(2):
            for u in range(2):
                start = pl.multiple_of((core if u == 0 else 1 - core) * 512 + first, LANES)
                place = outs[o].at[:, pl.ds((2 * t + u) * width, width)]
                for k in range(8):

                    @pl.when(places[2 * o + t] == k)
                    def _():
                        pltpu.make_async_copy(
                            blocks[k].at[:, pl.ds(start, width)], place, sems.at[4 * o + 2 * t + u]
                        ).start()

    for o in range(4):
        for q in range(4):
            place = outs[o].at[:, pl.ds(q * width, width)]
            pltpu.make_async_copy(blocks[0].at[:, pl.ds(0, width)], place, sems.at[4 * o + q]).wait()


def select(places, blocks, first, width, after=(), us=2.5):
    rows = blocks[0].shape[0]
    return pl.pallas_call(
        functools.partial(select_kernel, first, width),
        in_specs=[pl.BlockSpec(memory_space=pltpu.SMEM)] + any_specs(8 + len(after)),
        out_specs=[pl.BlockSpec(memory_space=pltpu.VMEM)] * 4,
        out_shape=[jax.ShapeDtypeStruct((rows, 4 * width), BF16)] * 4,
        scratch_shapes=[pltpu.SemaphoreType.DMA((16,))],
        compiler_params=pltpu.CompilerParams(vmem_limit_bytes=VMEM_LIMIT),
        cost_estimate=cost(us),
        name="select",
    )(places, *blocks, *after)


def weight_kernel(scale, q0, q1, q2, q3, g0, g1, g2, g3, *refs):
    keep, give = refs[-2:]
    width = g0.shape[1] // 4
    total = jnp.dot(q0[...], g0[...], preferred_element_type=F32)
    total = total + jnp.dot(q1[...], g1[...], preferred_element_type=F32)
    total = total + jnp.dot(q2[...], g2[...], preferred_element_type=F32)
    total = total + jnp.dot(q3[...], g3[...], preferred_element_type=F32)
    total = (total * scale).astype(BF16)
    for t in range(2):
        keep[t] = total[:, 2 * t * width : (2 * t + 1) * width]
        give[t] = total[:, (2 * t + 1) * width : (2 * t + 2) * width]


def weight_sum(left, got, scale, after=()):
    ch, n = left[0].shape
    width = got[0].shape[1] // 4
    tile = 256
    rows = pl.BlockSpec((tile, n), lambda i: (i, 0))
    right = pl.BlockSpec((n, 4 * width), lambda i: (0, 0))
    return pl.pallas_call(
        functools.partial(weight_kernel, scale),
        grid=(ch // tile,),
        in_specs=[rows] * 4 + [right] * 4 + any_specs(len(after)),
        out_specs=[pl.BlockSpec((2, tile, width), lambda i: (0, i, 0))] * 2,
        out_shape=[jax.ShapeDtypeStruct((2, ch, width), BF16)] * 2,
        compiler_params=pltpu.CompilerParams(vmem_limit_bytes=VMEM_LIMIT),
        cost_estimate=cost(0.2),
        name="weight_sum",
    )(*left, *got, *after)


def halo_kernel(q, k, v, out, sems):
    n = q.shape[0]
    copies = [
        pltpu.make_async_copy(q.at[n - HEAD :], out.at[:HEAD], sems.at[0]),
        pltpu.make_async_copy(k.at[n - HALO :], out.at[HEAD : HEAD + HALO], sems.at[1]),
        pltpu.make_async_copy(v.at[n - HALO :], out.at[HEAD + HALO :], sems.at[2]),
    ]
    for copy in copies:
        copy.start()
    for copy in copies:
        copy.wait()


def last_rows(q, k, v):
    return pl.pallas_call(
        halo_kernel,
        in_specs=[pl.BlockSpec(memory_space=pltpu.HBM)] * 3,
        out_specs=pl.BlockSpec(memory_space=pltpu.VMEM),
        out_shape=jax.ShapeDtypeStruct((HEAD + 2 * HALO, q.shape[1]), BF16),
        scratch_shapes=[pltpu.SemaphoreType.DMA((3,))],
        compiler_params=pltpu.CompilerParams(vmem_limit_bytes=VMEM_LIMIT),
        cost_estimate=cost(1),
        name="last_rows",
    )(q, k, v)


def wave_kernel(right, left, got, *refs):
    refs[-2][...] = right[...]
    refs[-1][...] = (left[...] + got[...].astype(F32)).astype(BF16)


def wave(right, left, got, after):
    rows, ch = right.shape
    spec = pl.BlockSpec((rows // 2, ch), lambda i: (i, 0))
    return pl.pallas_call(
        wave_kernel,
        grid=(2,),
        in_specs=[spec] * 3 + any_specs(len(after)),
        out_specs=[spec, spec],
        out_shape=[jax.ShapeDtypeStruct((rows, ch), BF16)] * 2,
        compiler_params=pltpu.CompilerParams(vmem_limit_bytes=VMEM_LIMIT),
        cost_estimate=cost(0.2),
        name="wave",
    )(right, left, got, *after)


def combine_kernel(kept, from_core, *refs):
    refs[-1][...] = (kept[0].astype(F32) + from_core[0].astype(F32)).astype(BF16)


def combine(kept, from_core, after):
    _, rows, width = kept.shape
    tile = 256
    second = pl.BlockSpec((1, tile, width), lambda i: (1, i, 0))
    return pl.pallas_call(
        combine_kernel,
        grid=(rows // tile,),
        in_specs=[second, second] + any_specs(len(after)),
        out_specs=pl.BlockSpec((tile, width), lambda i: (i, 0)),
        out_shape=jax.ShapeDtypeStruct((rows, width), BF16),
        compiler_params=pltpu.CompilerParams(vmem_limit_bytes=VMEM_LIMIT),
        cost_estimate=cost(0.2),
        name="combine",
    )(kept, from_core, *after)


def finish_kernel(kept, from_core, from_yl, *refs):
    total = kept[0].astype(F32) + from_core[0].astype(F32) + from_yl[...].astype(F32)
    refs[-1][...] = total.astype(BF16)


def finish(kept, from_core, from_yl, first, width, shape, us, before=()):
    tile = 256
    both = pl.BlockSpec((1, tile, width), lambda i: (0, i, 0))
    return pl.pallas_call(
        finish_kernel,
        grid=(shape[0] // tile,),
        in_specs=[both, both, pl.BlockSpec((tile, width), lambda i: (i, 0))] + any_specs(len(before)),
        out_specs=pl.BlockSpec((tile, width), lambda i: (i, first // width)),
        out_shape=jax.ShapeDtypeStruct(shape, BF16),
        input_output_aliases={3: 0} if before else {},
        compiler_params=pltpu.CompilerParams(vmem_limit_bytes=VMEM_LIMIT),
        cost_estimate=cost(us),
        name="finish",
    )(kept, from_core, from_yl, *before)


def on_device(query_in, key_in, value_in, short_filter, long_filter, skip_gain, out_weight, grad_output):
    n, ch = query_in.shape
    ctx, tp = lax.axis_index("ctx"), lax.axis_index("tp")
    z, yl, c = ctx // 4, (ctx // 2) % 2, ctx % 2
    yh, x = tp // 4, tp % 4
    gain = skip_gain.reshape(1, ch)
    w = out_weight

    own = grad_output
    r1, l1 = along_x(own, 1), along_x(own, -1)
    other = across_yh(own)
    halo = next_shard(last_rows(query_in, key_in, value_in), 1)
    r2, l2 = along_x(other, 1), along_x(other, -1)
    r3, l3 = along_x(r1, 1), along_x(l2, -1)

    taps = long_filter.astype(F32).T
    none = jnp.zeros((taps.shape[0], 1), F32)
    pad = jnp.zeros((taps.shape[0], taps.shape[1] - 1), F32)
    taps_fwd = jnp.concatenate([none, taps[:, ::-1], pad], axis=1)
    taps_bwd = jnp.concatenate([taps, none, pad], axis=1)
    query_conv, carried, key_conv, value_conv, gated, gated_t = forward(
        query_in, key_in, value_in, halo, short_filter, taps_fwd, gain, [other, r1, l1]
    )

    left = [gated_t, along_z(gated_t, 1), along_z(gated_t, -1), along_z(gated_t, 2)]

    def block_cols(dys, dxs):
        dy, dx = jnp.array(dys), jnp.array(dxs)
        return (((yh + dy) % YH) * X + (x + dx) % X).astype(jnp.int32)

    near_gg = grad_product(block_cols([0, 0, 1, 1], [3, 1, 3, 1]), [r1, l1, r2, l2], w)

    far_up, far_down = project(
        block_cols([1, 0], [2, 2]), gated, w, [BF16, BF16], after=near_gg
    )
    got_r, got_l = along_x(far_up, 1), along_x(far_down, -1)

    plane = (z + jnp.array([0, 1, 3, 2])) % Z
    parity = (yl + jnp.array([0, 1])) % 2
    to_x = (2 * (plane % 2))[:, None] + parity[None]
    dy, dx = (plane // 2 + yh) % 2, (to_x - x) % X
    places = jnp.array([0, 2, 6, 1, 3, 5, 7, 4])[dy[:, None] * 4 + dx].reshape(8)
    places = jnp.concatenate([places, c[None]]).astype(jnp.int32)
    blocks = [own, r1, l1, other, r2, l2, r3, l3]
    splits = [(0, 256), (256, 256)]
    first = select(places, blocks, *splits[0], after=[far_up])

    right1, left1 = project(block_cols([1, 1], [1, 3]), gated, w, [F32, BF16], after=[first[0], *left], us=6)
    right0, left0, stay0, stay1 = project(
        block_cols([0, 0, 0, 1], [1, 3, 0, 0]), gated, w, [BF16, F32, F32, F32], after=[left1, *left], us=8
    )
    grad_carried, grad_query_conv, rim = grad_product(
        block_cols([0, 0, 1, 1], [0, 2, 0, 2]), [own, r3, other, l3], w,
        (near_gg[0], query_conv, carried, value_conv, key_conv), after=[stay1, got_r, got_l], us=0.2,
    )
    rim = next_shard(rim, -1)
    second = select(places, blocks, *splits[1], after=[grad_carried], us=0.2)

    from_r1 = along_x((right1.astype(F32) + got_r.astype(F32)).astype(BF16), 1)
    from_l1 = along_x(left1, -1)
    swap = (stay1 + from_r1.astype(F32) + from_l1.astype(F32)).astype(BF16)
    swapped = across_yh(swap)

    grad_query, grad_key, grad_value = backward(
        grad_carried, grad_query_conv, value_conv, key_conv, rim,
        short_filter, taps_bwd, gain, [from_r1, from_l1],
    )

    scale = float(n * Z * YL * CORE) ** -0.5
    after, done = [second[0], from_r1, from_l1], []
    waves = []
    for (keep, up, down, across), split, us in zip((first, second), splits, (20, 1)):
        got = [keep, along_z(up, 1), along_z(down, -1), along_z(across, 2)]
        kept, given = weight_sum(left, got, scale, after)
        from_core = across_core(given)
        total = combine(kept, from_core, done)
        waves = waves or wave(right0, left0, got_l, [total])
        after = [total, grad_query]
        done = [finish(kept, from_core, across_yl(total), *split, (ch, 512), us, done)]

    from_r0, from_l0 = along_x(waves[0], 1), along_x(waves[1], -1)
    output = stay0 + from_r0.astype(F32) + from_l0.astype(F32) + swapped.astype(F32)
    output = output.astype(BF16)
    return output, grad_query, grad_key, grad_value, done[0]


def solution(mesh):
    return jax.shard_map(
        on_device,
        mesh=mesh,
        in_specs=(
            P("ctx", "tp"),
            P("ctx", "tp"),
            P("ctx", "tp"),
            P(None, None, "tp"),
            P(None, "tp"),
            P("tp"),
            P("tp", None),
            P("ctx", "tp"),
        ),
        out_specs=(P("ctx", "tp"), P("ctx", "tp"), P("ctx", "tp"), P("ctx", "tp"), P("tp", "ctx")),
        check_vma=False,
    )
```

```python
import functools

import jax
import jax.numpy as jnp
from jax import lax
from jax.experimental import pallas as pl
from jax.experimental.pallas import tpu as pltpu
from jax.sharding import PartitionSpec as P

Z, YL, CORE, YH, X = 4, 2, 2, 2, 4
F32, BF16 = jnp.float32, jnp.bfloat16
HALO = 144
HEAD = 16
LANES = 128
VMEM_LIMIT = 16 * 1024 * 1024
VMEM_ALL = 60 * 1024 * 1024
VMEM_MOST = 50 * 1024 * 1024


def cost(us):
    return pl.CostEstimate(flops=int(us * 4.6e9), bytes_accessed=2**16, transcendentals=0)


def ctx_pairs(move):
    pairs = []
    for i in range(Z * YL * CORE):
        z, yl, c = move(i // 4, (i // 2) % 2, i % 2)
        pairs.append((i, (z % Z) * 4 + (yl % YL) * 2 + c % CORE))
    return pairs


def tp_pairs(move):
    pairs = []
    for j in range(YH * X):
        yh, x = move(j // 4, j % 4)
        pairs.append((j, (yh % YH) * 4 + x % X))
    return pairs


def along_x(a, d):
    return lax.ppermute(a, "tp", tp_pairs(lambda yh, x: (yh, x + d)))


def across_yh(a):
    return lax.ppermute(a, "tp", tp_pairs(lambda yh, x: (yh + 1, x)))


def along_z(a, d):
    return lax.ppermute(a, "ctx", ctx_pairs(lambda z, yl, c: (z + d, yl, c)))


def across_core(a):
    return lax.ppermute(a, "ctx", ctx_pairs(lambda z, yl, c: (z, yl, c + 1)))


def next_shard(a, d):
    n = Z * YL * CORE
    return lax.ppermute(a, "ctx", [(i, i + d) for i in range(n) if 0 <= i + d < n])


def across_yl(a):
    return lax.ppermute(a, "ctx", ctx_pairs(lambda z, yl, c: (z, yl + 1, c)))


def any_specs(n):
    return [pl.BlockSpec(memory_space=pl.ANY)] * n


def toeplitz_into(table, rows):
    for g in range(8):
        wide = jnp.broadcast_to(rows[g : g + 1, :], (LANES, 2 * LANES))
        table[g * LANES : (g + 1) * LANES, :] = pltpu.roll(
            wide, 0, 1, stride=1, stride_axis=0
        ).astype(BF16)


def pick_groups(res, rows):
    lane_group = (lax.broadcasted_iota(jnp.int32, (rows, res.shape[1]), 1) % LANES) // 16
    out = res[:rows]
    for g in range(1, 8):
        out = jnp.where(lane_group == g, res[g * rows : (g + 1) * rows], out)
    return out


def forward_kernel(
    q, k, v, halo, sf, taps, gain, *refs
):
    qc_o, ca_o, kc_o, vc_o, qg_o, qgt_o, qs, ks, vs, table = refs[-10:]
    n = q.shape[0]
    qs[:HEAD] = halo[:HEAD].astype(F32)
    qs[HEAD:] = q[...].astype(F32)
    ks[:HEAD] = halo[HEAD : 2 * HEAD].astype(F32)
    ks[HEAD:] = k[...].astype(F32)
    vs[:HEAD] = halo[2 * HEAD : 3 * HEAD].astype(F32)
    vs[HEAD:] = v[...].astype(F32)
    toeplitz_into(table, taps[...])

    def short(scr, member, first, rows):
        acc = sf[member, 0:1, :] * scr[pl.ds(first, rows), :]
        for s in range(1, 7):
            acc = acc + sf[member, s : s + 1, :] * scr[pl.ds(first - s, rows), :]
        return acc

    qc = short(qs, 0, HEAD, n)
    kc = short(ks, 1, HEAD, n)
    vc = short(vs, 2, HEAD, n)
    kv = jnp.concatenate([halo[3 * HEAD :], (kc * vc).astype(BF16)], axis=0)
    window = jnp.concatenate([kv[: 2 * LANES], kv[LANES:]], axis=1)
    res = pick_groups(jnp.dot(table[...], window, preferred_element_type=F32), LANES)
    carried = jnp.concatenate([res[:, :LANES], res[:, LANES:]], axis=0)
    carried = carried + gain[...] * kv[LANES:].astype(F32)
    qc_o[...] = qc
    ca_o[...] = carried
    kc_o[...] = kc
    vc_o[...] = vc
    gated = qc * carried
    qg_o[...] = gated.astype(BF16)
    qgt_o[...] = gated.T.astype(BF16)


def forward(q, k, v, halo, sf, taps, gain, after):
    n, ch = q.shape
    col = lambda rows: pl.BlockSpec((rows, LANES), lambda i: (0, i))
    return pl.pallas_call(
        forward_kernel,
        grid=(ch // LANES,),
        in_specs=[
            col(n), col(n), col(n), col(3 * HEAD + LANES),
            pl.BlockSpec((3, 7, LANES), lambda i: (0, 0, i)),
            pl.BlockSpec((8, 2 * LANES), lambda i: (i, 0)),
            col(1),
        ]
        + [pl.BlockSpec(memory_space=pl.ANY)] * len(after),
        out_specs=[col(n)] * 5 + [pl.BlockSpec((LANES, n), lambda i: (i, 0))],
        out_shape=[jax.ShapeDtypeStruct((n, ch), F32)] * 4
        + [jax.ShapeDtypeStruct((n, ch), BF16), jax.ShapeDtypeStruct((ch, n), BF16)],
        scratch_shapes=[
            pltpu.VMEM((HEAD + n, LANES), F32),
            pltpu.VMEM((HEAD + n, LANES), F32),
            pltpu.VMEM((HEAD + n, LANES), F32),
            pltpu.VMEM((8 * LANES, 2 * LANES), BF16),
        ],
        compiler_params=pltpu.CompilerParams(vmem_limit_bytes=VMEM_ALL),
        cost_estimate=cost(8),
        name="forward",
    )(q, k, v, halo, sf, taps, gain, *after)


def backward_kernel(gc, gq, vc, kc, rim, sf, taps, gain, *refs):
    dq_o, dk_o, dv_o, gs, qs, ks, vs, table = refs[-8:]
    n = gc.shape[0]
    gs[:n] = gc[...]
    gs[n : n + HALO] = rim[:HALO]
    gs[n + HALO :] = jnp.zeros((gs.shape[0] - n - HALO, LANES), BF16)
    toeplitz_into(table, taps[...])
    window = jnp.concatenate([gs[: 2 * LANES], gs[LANES : 3 * LANES]], axis=1)
    res = pick_groups(jnp.dot(table[...], window, preferred_element_type=F32), LANES)
    small = jnp.concatenate([table[g * LANES : g * LANES + HEAD] for g in range(8)], axis=0)
    tail = pick_groups(jnp.dot(small, gs[2 * LANES :], preferred_element_type=F32), HEAD)
    gp = jnp.concatenate([res[:, :LANES], res[:, LANES:]], axis=0) + gain[...] * gs[:n].astype(F32)
    gp_tail = tail + gain[...] * gs[n : n + HEAD].astype(F32)
    qs[:n] = gq[...]
    qs[n:] = rim[HALO + 0 * HEAD : HALO + 1 * HEAD].astype(F32)
    ks[:n] = gp * vc[...]
    ks[n:] = gp_tail * rim[HALO + 1 * HEAD : HALO + 2 * HEAD].astype(F32)
    vs[:n] = gp * kc[...]
    vs[n:] = gp_tail * rim[HALO + 2 * HEAD : HALO + 3 * HEAD].astype(F32)

    def short(scr, member):
        acc = sf[member, 0:1, :] * scr[pl.ds(0, n), :]
        for s in range(1, 7):
            acc = acc + sf[member, s : s + 1, :] * scr[pl.ds(s, n), :]
        return acc.astype(BF16)

    dq_o[...] = short(qs, 0)
    dk_o[...] = short(ks, 1)
    dv_o[...] = short(vs, 2)


def backward(gc, gq, vc, kc, rim, sf, taps, gain, after):
    n, ch = gc.shape
    col = lambda rows: pl.BlockSpec((rows, LANES), lambda i: (0, i))
    return pl.pallas_call(
        backward_kernel,
        grid=(ch // LANES,),
        in_specs=[
            col(n), col(n), col(n), col(n), col(HALO + 3 * HEAD),
            pl.BlockSpec((3, 7, LANES), lambda i: (0, 0, i)),
            pl.BlockSpec((8, 2 * LANES), lambda i: (i, 0)),
            col(1),
        ]
        + any_specs(len(after)),
        out_specs=[col(n)] * 3,
        out_shape=[jax.ShapeDtypeStruct((n, ch), BF16)] * 3,
        scratch_shapes=[
            pltpu.VMEM((4 * LANES, LANES), BF16),
            pltpu.VMEM((n + HEAD, LANES), F32),
            pltpu.VMEM((n + HEAD, LANES), F32),
            pltpu.VMEM((n + HEAD, LANES), F32),
            pltpu.VMEM((8 * LANES, 2 * LANES), BF16),
        ],
        compiler_params=pltpu.CompilerParams(vmem_limit_bytes=VMEM_LIMIT),
        cost_estimate=cost(8),
        name="backward",
    )(gc, gq, vc, kc, rim, sf, taps, gain, *after)


def grad_kernel(n_blocks, last, cols, *refs):
    blocks, w = refs[:n_blocks], refs[n_blocks]
    acc = refs[-1]
    i = pl.program_id(0)
    for k in range(n_blocks):

        @pl.when(i == k)
        def _():
            part = lax.dot_general(
                blocks[k][...], w[...], (((1,), (1,)), ((), ())), preferred_element_type=F32
            )
            if k == 0 and last:
                acc[...] = part + refs[n_blocks + 1][...]
            elif k == 0:
                acc[...] = part
            else:
                acc[...] += part

    if not last:

        @pl.when(i == n_blocks - 1)
        def _():
            refs[-2][...] = acc[...]

        return

    query_conv, carried, value_conv, key_conv = refs[n_blocks + 2 : n_blocks + 6]
    gc_o, gq_o, rim_o = refs[-4:-1]

    @pl.when(i == n_blocks - 1)
    def _():
        grad_carried = (acc[...] * query_conv[...]).astype(BF16)
        gc_o[...] = grad_carried
        gq = acc[...] * carried[...]
        gq_o[...] = gq
        rim_o[:HALO] = grad_carried[:HALO]
        for k, rows in enumerate((gq, value_conv, key_conv)):
            rim_o[HALO + k * HEAD : HALO + (k + 1) * HEAD] = rows[:HEAD].astype(BF16)


def grad_product(cols, blocks, w, rest=(), after=(), us=6.4):
    n = len(blocks)
    rows, width = blocks[0].shape
    ch = w.shape[0]
    whole = lambda r: pl.BlockSpec((r, ch), lambda i, s: (0, 0))
    if rest:
        outs = [
            jax.ShapeDtypeStruct((rows, ch), BF16),
            jax.ShapeDtypeStruct((rows, ch), F32),
            jax.ShapeDtypeStruct((HALO + 3 * HEAD, ch), BF16),
        ]
        rest_specs = [whole(rows)] * 3 + [whole(HEAD)] * 2
    else:
        outs, rest_specs = [jax.ShapeDtypeStruct((rows, ch), F32)], []
    return pl.pallas_call(
        functools.partial(grad_kernel, n, bool(rest)),
        grid_spec=pltpu.PrefetchScalarGridSpec(
            num_scalar_prefetch=1,
            grid=(n,),
            in_specs=[whole(rows)] * n
            + [pl.BlockSpec((ch, width), lambda i, s: (0, s[i]))]
            + rest_specs
            + any_specs(len(after)),
            out_specs=[whole(o.shape[0]) for o in outs],
            scratch_shapes=[pltpu.VMEM((rows, ch), F32)],
        ),
        out_shape=outs,
        compiler_params=pltpu.CompilerParams(vmem_limit_bytes=VMEM_MOST),
        cost_estimate=cost(us),
        name="grad_product",
    )(cols, *blocks, w, *rest, *after)


def project_kernel(n, cols, qg, w, *refs):
    i = pl.program_id(0)
    part = jnp.dot(qg[...], w[...], preferred_element_type=F32)
    for k in range(n):

        @pl.when(i == k)
        def _():
            refs[k - n][...] = part.astype(refs[k - n].dtype)


def project(cols, qg, w, kinds, after=(), us=3.2):
    n = len(kinds)
    rows, ch = qg.shape
    whole = pl.BlockSpec((rows, ch), lambda i, s: (0, 0))
    return pl.pallas_call(
        functools.partial(project_kernel, n),
        grid_spec=pltpu.PrefetchScalarGridSpec(
            num_scalar_prefetch=1,
            grid=(n,),
            in_specs=[whole, pl.BlockSpec((ch, ch), lambda i, s: (0, s[i]))] + any_specs(len(after)),
            out_specs=[whole] * n,
        ),
        out_shape=[jax.ShapeDtypeStruct((rows, ch), kind) for kind in kinds],
        compiler_params=pltpu.CompilerParams(vmem_limit_bytes=VMEM_MOST),
        cost_estimate=cost(us),
        name="project",
    )(cols, qg, w, *after)


def select_kernel(first, width, places, *refs):
    blocks, outs, sems = refs[:8], refs[-5:-1], refs[-1]
    core = places[8]
    for o in range(4):
        for t in range(2):
            for u in range(2):
                start = pl.multiple_of((core if u == 0 else 1 - core) * 512 + first, LANES)
                place = outs[o].at[:, pl.ds((2 * t + u) * width, width)]
                for k in range(8):

                    @pl.when(places[2 * o + t] == k)
                    def _():
                        pltpu.make_async_copy(
                            blocks[k].at[:, pl.ds(start, width)], place, sems.at[4 * o + 2 * t + u]
                        ).start()

    for o in range(4):
        for q in range(4):
            place = outs[o].at[:, pl.ds(q * width, width)]
            pltpu.make_async_copy(blocks[0].at[:, pl.ds(0, width)], place, sems.at[4 * o + q]).wait()


def select(places, blocks, first, width, after=(), us=2.5):
    rows = blocks[0].shape[0]
    return pl.pallas_call(
        functools.partial(select_kernel, first, width),
        in_specs=[pl.BlockSpec(memory_space=pltpu.SMEM)] + any_specs(8 + len(after)),
        out_specs=[pl.BlockSpec(memory_space=pltpu.VMEM)] * 4,
        out_shape=[jax.ShapeDtypeStruct((rows, 4 * width), BF16)] * 4,
        scratch_shapes=[pltpu.SemaphoreType.DMA((16,))],
        compiler_params=pltpu.CompilerParams(vmem_limit_bytes=VMEM_LIMIT),
        cost_estimate=cost(us),
        name="select",
    )(places, *blocks, *after)


def weight_kernel(scale, q0, q1, q2, q3, g0, g1, g2, g3, *refs):
    keep, give = refs[-2:]
    width = g0.shape[1] // 4
    total = jnp.dot(q0[...], g0[...], preferred_element_type=F32)
    total = total + jnp.dot(q1[...], g1[...], preferred_element_type=F32)
    total = total + jnp.dot(q2[...], g2[...], preferred_element_type=F32)
    total = total + jnp.dot(q3[...], g3[...], preferred_element_type=F32)
    total = (total * scale).astype(BF16)
    for t in range(2):
        keep[t] = total[:, 2 * t * width : (2 * t + 1) * width]
        give[t] = total[:, (2 * t + 1) * width : (2 * t + 2) * width]


def weight_sum(left, got, scale, after=()):
    ch, n = left[0].shape
    width = got[0].shape[1] // 4
    tile = 256
    rows = pl.BlockSpec((tile, n), lambda i: (i, 0))
    right = pl.BlockSpec((n, 4 * width), lambda i: (0, 0))
    return pl.pallas_call(
        functools.partial(weight_kernel, scale),
        grid=(ch // tile,),
        in_specs=[rows] * 4 + [right] * 4 + any_specs(len(after)),
        out_specs=[pl.BlockSpec((2, tile, width), lambda i: (0, i, 0))] * 2,
        out_shape=[jax.ShapeDtypeStruct((2, ch, width), BF16)] * 2,
        compiler_params=pltpu.CompilerParams(vmem_limit_bytes=VMEM_LIMIT),
        cost_estimate=cost(0.2),
        name="weight_sum",
    )(*left, *got, *after)


def last_rows_kernel(q, k_before, k, v_before, v, sf, out, ks, vs):
    for scratch, before, tail in ((ks, k_before, k), (vs, v_before, v)):
        scratch[:HEAD] = before[...].astype(F32)
        scratch[HEAD:] = tail[...].astype(F32)
    rows = k.shape[0]
    kc = sf[1, 0:1, :] * ks[HEAD:]
    vc = sf[2, 0:1, :] * vs[HEAD:]
    for s in range(1, 7):
        kc = kc + sf[1, s : s + 1, :] * ks[pl.ds(HEAD - s, rows), :]
        vc = vc + sf[2, s : s + 1, :] * vs[pl.ds(HEAD - s, rows), :]
    out[:HEAD] = q[...]
    out[HEAD : 2 * HEAD] = k[rows - HEAD :]
    out[2 * HEAD : 3 * HEAD] = v[rows - HEAD :]
    out[3 * HEAD :] = (kc * vc).astype(BF16)


def last_rows(q, k, v, sf):
    n, ch = q.shape
    width = 512
    part = lambda rows, i: pl.BlockSpec((rows, width), lambda j: (i, j))
    tail = part(LANES, n // LANES - 1)
    before = part(HEAD, (n - LANES) // HEAD - 1)
    return pl.pallas_call(
        last_rows_kernel,
        grid=(ch // width,),
        in_specs=[part(HEAD, n // HEAD - 1), before, tail, before, tail]
        + [pl.BlockSpec((3, 7, width), lambda j: (0, 0, j))],
        out_specs=part(3 * HEAD + LANES, 0),
        out_shape=jax.ShapeDtypeStruct((3 * HEAD + LANES, ch), BF16),
        scratch_shapes=[pltpu.VMEM((HEAD + LANES, width), F32)] * 2,
        compiler_params=pltpu.CompilerParams(vmem_limit_bytes=VMEM_ALL),
        cost_estimate=cost(1),
        name="last_rows",
    )(q, k, k, v, v, sf)


def wave_kernel(right, left, got, *refs):
    refs[-2][...] = right[...]
    refs[-1][...] = (left[...] + got[...].astype(F32)).astype(BF16)


def wave(right, left, got, after):
    rows, ch = right.shape
    spec = pl.BlockSpec((rows // 2, ch), lambda i: (i, 0))
    return pl.pallas_call(
        wave_kernel,
        grid=(2,),
        in_specs=[spec] * 3 + any_specs(len(after)),
        out_specs=[spec, spec],
        out_shape=[jax.ShapeDtypeStruct((rows, ch), BF16)] * 2,
        compiler_params=pltpu.CompilerParams(vmem_limit_bytes=VMEM_LIMIT),
        cost_estimate=cost(8),
        name="wave",
    )(right, left, got, *after)


def combine_kernel(kept, from_core, *refs):
    refs[-1][...] = (kept[0].astype(F32) + from_core[0].astype(F32)).astype(BF16)


def combine(kept, from_core, after, us):
    _, rows, width = kept.shape
    tile = 256
    second = pl.BlockSpec((1, tile, width), lambda i: (1, i, 0))
    return pl.pallas_call(
        combine_kernel,
        grid=(rows // tile,),
        in_specs=[second, second] + any_specs(len(after)),
        out_specs=pl.BlockSpec((tile, width), lambda i: (i, 0)),
        out_shape=jax.ShapeDtypeStruct((rows, width), BF16),
        compiler_params=pltpu.CompilerParams(vmem_limit_bytes=VMEM_LIMIT),
        cost_estimate=cost(us),
        name="combine",
    )(kept, from_core, *after)


def finish_kernel(kept, from_core, from_yl, *refs):
    before, out = refs[:-1], refs[-1]
    width = from_yl.shape[1]
    total = kept[0].astype(F32) + from_core[0].astype(F32) + from_yl[...].astype(F32)
    if before:
        out[:, :-width] = before[0][...]
        out[:, -width:] = total.astype(BF16)
    else:
        out[...] = total.astype(BF16)


def finish(kept, from_core, from_yl, us, before=()):
    tile = 256
    rows, width = from_yl.shape
    both = pl.BlockSpec((1, tile, width), lambda i: (0, i, 0))
    plain = lambda a: pl.BlockSpec((tile, a.shape[1]), lambda i: (i, 0))
    total = width + sum(a.shape[1] for a in before)
    return pl.pallas_call(
        finish_kernel,
        grid=(rows // tile,),
        in_specs=[both, both, plain(from_yl)] + [plain(a) for a in before],
        out_specs=pl.BlockSpec((tile, total), lambda i: (i, 0)),
        out_shape=jax.ShapeDtypeStruct((rows, total), BF16),
        compiler_params=pltpu.CompilerParams(vmem_limit_bytes=VMEM_LIMIT),
        cost_estimate=cost(us),
        name="finish",
    )(kept, from_core, from_yl, *before)


def on_device(query_in, key_in, value_in, short_filter, long_filter, skip_gain, out_weight, grad_output):
    n, ch = query_in.shape
    ctx, tp = lax.axis_index("ctx"), lax.axis_index("tp")
    z, yl, c = ctx // 4, (ctx // 2) % 2, ctx % 2
    yh, x = tp // 4, tp % 4
    gain = skip_gain.reshape(1, ch)
    w = out_weight

    own = grad_output
    r1, l1 = along_x(own, 1), along_x(own, -1)
    other = across_yh(own)
    halo = next_shard(last_rows(query_in, key_in, value_in, short_filter), 1)
    taps = long_filter.astype(F32).T
    none = jnp.zeros((taps.shape[0], 1), F32)
    pad = jnp.zeros((taps.shape[0], taps.shape[1] - 1), F32)
    taps_fwd = jnp.concatenate([none, taps[:, ::-1], pad], axis=1)
    taps_bwd = jnp.concatenate([taps, none, pad], axis=1)
    query_conv, carried, key_conv, value_conv, gated, gated_t = forward(
        query_in, key_in, value_in, halo, short_filter, taps_fwd, gain, [other, r1, l1]
    )

    r2, l2 = along_x(other, 1), along_x(other, -1)
    after_r2, _ = lax.optimization_barrier((r1, r2))
    r3, l3 = along_x(after_r2, 1), along_x(l2, -1)

    left = [gated_t, along_z(gated_t, 1), along_z(gated_t, -1), along_z(gated_t, 2)]

    def block_cols(dys, dxs):
        dy, dx = jnp.array(dys), jnp.array(dxs)
        return (((yh + dy) % YH) * X + (x + dx) % X).astype(jnp.int32)

    near_gg = grad_product(block_cols([0, 0, 1, 1], [3, 1, 3, 1]), [r1, l1, r2, l2], w)

    far_up, far_down = project(
        block_cols([1, 0], [2, 2]), gated, w, [BF16, BF16], after=near_gg
    )
    got_r, got_l = along_x(far_up, 1), along_x(far_down, -1)

    plane = (z + jnp.array([0, 1, 3, 2])) % Z
    parity = (yl + jnp.array([0, 1])) % 2
    to_x = (2 * (plane % 2))[:, None] + parity[None]
    dy, dx = (plane // 2 + yh) % 2, (to_x - x) % X
    places = jnp.array([0, 2, 6, 1, 3, 5, 7, 4])[dy[:, None] * 4 + dx].reshape(8)
    places = jnp.concatenate([places, c[None]]).astype(jnp.int32)
    blocks = [own, r1, l1, other, r2, l2, r3, l3]
    splits = [(0, 384), (384, 128)]
    first = select(places, blocks, *splits[0], after=[far_up])

    right1, left1 = project(block_cols([1, 1], [1, 3]), gated, w, [F32, BF16], after=[first[0], *left], us=6)
    right0, left0, stay0, stay1 = project(
        block_cols([0, 0, 0, 1], [1, 3, 0, 0]), gated, w, [BF16, F32, F32, F32], after=[left1, got_r, got_l, *left], us=8
    )
    second = select(places, blocks, *splits[1], after=[stay1], us=0.2)
    grad_carried, grad_query_conv, rim = grad_product(
        block_cols([0, 0, 1, 1], [0, 2, 0, 2]), [own, r3, other, l3], w,
        (near_gg[0], query_conv, carried, value_conv, key_conv), after=[second[0]], us=0.2,
    )

    from_r1 = along_x((right1.astype(F32) + got_r.astype(F32)).astype(BF16), 1)
    from_l1 = along_x(left1, -1)
    swap = (stay1 + from_r1.astype(F32) + from_l1.astype(F32)).astype(BF16)
    swapped = across_yh(swap)

    scale = float(n * Z * YL * CORE) ** -0.5

    *second, _ = lax.optimization_barrier((*second, swap))
    rim, _ = lax.optimization_barrier((rim, swap))
    rim = next_shard(rim, -1)

    def over_z(keep, up, down, across):
        return [keep, along_z(up, 1), along_z(down, -1), along_z(across, 2)]

    kept_a, given_a = weight_sum(left, over_z(*first), scale, [grad_carried, swap])
    core_a = across_core(given_a)
    waves = wave(right0, left0, got_l, [kept_a])
    sent_a = combine(kept_a, core_a, [waves[0]], 0.2)
    grad_query, grad_key, grad_value = backward(
        grad_carried, grad_query_conv, value_conv, key_conv, rim,
        short_filter, taps_bwd, gain, [swapped, sent_a],
    )
    kept_b, given_b = weight_sum(left, over_z(*second), scale, [grad_query])
    done_a = finish(kept_a, core_a, across_yl(sent_a), 20)
    core_b = across_core(given_b)
    sent_b = combine(kept_b, core_b, [done_a], 0.2)
    weight_grad = finish(kept_b, core_b, across_yl(sent_b), 1, [done_a])

    *waves, _ = lax.optimization_barrier((*waves, grad_query))
    from_r0, from_l0 = along_x(waves[0], 1), along_x(waves[1], -1)
    output = stay0 + from_r0.astype(F32) + from_l0.astype(F32) + swapped.astype(F32)
    output = output.astype(BF16)
    return output, grad_query, grad_key, grad_value, weight_grad


def solution(mesh):
    return jax.shard_map(
        on_device,
        mesh=mesh,
        in_specs=(
            P("ctx", "tp"),
            P("ctx", "tp"),
            P("ctx", "tp"),
            P(None, None, "tp"),
            P(None, "tp"),
            P("tp"),
            P("tp", None),
            P("ctx", "tp"),
        ),
        out_specs=(P("ctx", "tp"), P("ctx", "tp"), P("ctx", "tp"), P("ctx", "tp"), P("tp", "ctx")),
        check_vma=False,
    )
```

```python
import functools

import jax
import jax.numpy as jnp
from jax import lax
from jax.experimental import pallas as pl
from jax.experimental.pallas import tpu as pltpu
from jax.sharding import PartitionSpec as P

Z, YL, CORE, YH, X = 4, 2, 2, 2, 4
F32, BF16 = jnp.float32, jnp.bfloat16
HALO = 144
HEAD = 16
LANES = 128
PARTS = 4
VMEM_LIMIT = 16 * 1024 * 1024
VMEM_ALL = 60 * 1024 * 1024
VMEM_MOST = 50 * 1024 * 1024


def cost(us):
    return pl.CostEstimate(flops=int(us * 4.6e9), bytes_accessed=2**16, transcendentals=0)


def ctx_pairs(move):
    pairs = []
    for i in range(Z * YL * CORE):
        z, yl, c = move(i // 4, (i // 2) % 2, i % 2)
        pairs.append((i, (z % Z) * 4 + (yl % YL) * 2 + c % CORE))
    return pairs


def tp_pairs(move):
    pairs = []
    for j in range(YH * X):
        yh, x = move(j // 4, j % 4)
        pairs.append((j, (yh % YH) * 4 + x % X))
    return pairs


def along_x(a, d):
    return lax.ppermute(a, "tp", tp_pairs(lambda yh, x: (yh, x + d)))


def across_yh(a):
    return lax.ppermute(a, "tp", tp_pairs(lambda yh, x: (yh + 1, x)))


def along_z(a, d):
    return lax.ppermute(a, "ctx", ctx_pairs(lambda z, yl, c: (z + d, yl, c)))


def across_core(a):
    return lax.ppermute(a, "ctx", ctx_pairs(lambda z, yl, c: (z, yl, c + 1)))


def next_shard(a, d):
    n = Z * YL * CORE
    return lax.ppermute(a, "ctx", [(i, i + d) for i in range(n) if 0 <= i + d < n])


def across_yl(a):
    return lax.ppermute(a, "ctx", ctx_pairs(lambda z, yl, c: (z, yl + 1, c)))


def any_specs(n):
    return [pl.BlockSpec(memory_space=pl.ANY)] * n


def toeplitz_into(table, rows):
    for g in range(8):
        wide = jnp.broadcast_to(rows[g : g + 1, :], (LANES, 2 * LANES))
        table[g * LANES : (g + 1) * LANES, :] = pltpu.roll(
            wide, 0, 1, stride=1, stride_axis=0
        ).astype(BF16)


def pick_groups(res, rows):
    lane_group = (lax.broadcasted_iota(jnp.int32, (rows, res.shape[1]), 1) % LANES) // 16
    out = res[:rows]
    for g in range(1, 8):
        out = jnp.where(lane_group == g, res[g * rows : (g + 1) * rows], out)
    return out


def table_kernel(taps, out):
    toeplitz_into(out, taps[...])


def toeplitz_table(taps):
    groups, window = taps.shape
    return pl.pallas_call(
        table_kernel,
        grid=(groups // 8,),
        in_specs=[pl.BlockSpec((8, window), lambda i: (i, 0))],
        out_specs=pl.BlockSpec((8 * LANES, window), lambda i: (i, 0)),
        out_shape=jax.ShapeDtypeStruct((groups * LANES, window), BF16),
        compiler_params=pltpu.CompilerParams(vmem_limit_bytes=VMEM_LIMIT),
        cost_estimate=cost(6),
        name="toeplitz_table",
    )(taps)


def forward_kernel(q, k, v, halo, sf, table, gain, *refs):
    outs, scratch = refs[-9:-3], refs[-3:]
    for part in range(PARTS):
        lanes, rows = pl.ds(part * LANES, LANES), pl.ds(part * 8 * LANES, 8 * LANES)
        forward_part(
            *[a.at[:, lanes] for a in (q, k, v, halo)], sf.at[:, :, lanes], table.at[rows], gain.at[:, lanes],
            *[a.at[:, lanes] for a in outs[:5]], outs[5].at[lanes], *scratch,
        )


def forward_part(q, k, v, halo, sf, table, gain, qc_o, ca_o, kc_o, vc_o, qg_o, qgt_o, qs, ks, vs):
    n = q.shape[0]
    qs[:HEAD] = halo[:HEAD].astype(F32)
    qs[HEAD:] = q[...].astype(F32)
    ks[:HEAD] = halo[HEAD : 2 * HEAD].astype(F32)
    ks[HEAD:] = k[...].astype(F32)
    vs[:HEAD] = halo[2 * HEAD : 3 * HEAD].astype(F32)
    vs[HEAD:] = v[...].astype(F32)

    def short(scr, member, first, rows):
        acc = sf[member, 0:1, :] * scr[pl.ds(first, rows), :]
        for s in range(1, 7):
            acc = acc + sf[member, s : s + 1, :] * scr[pl.ds(first - s, rows), :]
        return acc

    qc = short(qs, 0, HEAD, n)
    kc = short(ks, 1, HEAD, n)
    vc = short(vs, 2, HEAD, n)
    kv = jnp.concatenate([halo[3 * HEAD :], (kc * vc).astype(BF16)], axis=0)
    window = jnp.concatenate([kv[: 2 * LANES], kv[LANES:]], axis=1)
    res = pick_groups(jnp.dot(table[...], window, preferred_element_type=F32), LANES)
    carried = jnp.concatenate([res[:, :LANES], res[:, LANES:]], axis=0)
    carried = carried + gain[...] * kv[LANES:].astype(F32)
    qc_o[...] = qc
    ca_o[...] = carried
    kc_o[...] = kc
    vc_o[...] = vc
    gated = qc * carried
    qg_o[...] = gated.astype(BF16)
    qgt_o[...] = gated.T.astype(BF16)


def forward(q, k, v, halo, sf, table, gain, after):
    n, ch = q.shape
    col = lambda rows: pl.BlockSpec((rows, PARTS * LANES), lambda i: (0, i))
    return pl.pallas_call(
        forward_kernel,
        grid=(ch // LANES // PARTS,),
        in_specs=[
            col(n), col(n), col(n), col(3 * HEAD + LANES),
            pl.BlockSpec((3, 7, PARTS * LANES), lambda i: (0, 0, i)),
            pl.BlockSpec((PARTS * 8 * LANES, 2 * LANES), lambda i: (i, 0)),
            col(1),
        ]
        + [pl.BlockSpec(memory_space=pl.ANY)] * len(after),
        out_specs=[col(n)] * 5 + [pl.BlockSpec((PARTS * LANES, n), lambda i: (i, 0))],
        out_shape=[jax.ShapeDtypeStruct((n, ch), F32)] * 4
        + [jax.ShapeDtypeStruct((n, ch), BF16), jax.ShapeDtypeStruct((ch, n), BF16)],
        scratch_shapes=[
            pltpu.VMEM((HEAD + n, LANES), F32),
            pltpu.VMEM((HEAD + n, LANES), F32),
            pltpu.VMEM((HEAD + n, LANES), F32),
        ],
        compiler_params=pltpu.CompilerParams(vmem_limit_bytes=VMEM_ALL),
        cost_estimate=cost(8),
        name="forward",
    )(q, k, v, halo, sf, table, gain, *after)


def backward_kernel(gc, gq, vc, kc, rim, sf, taps, gain, *refs):
    outs, scratch = refs[-8:-5], refs[-5:]
    for part in range(PARTS):
        lanes, rows = pl.ds(part * LANES, LANES), pl.ds(part * 8, 8)
        backward_part(
            *[a.at[:, lanes] for a in (gc, gq, vc, kc, rim)], sf.at[:, :, lanes], taps.at[rows],
            gain.at[:, lanes], *[a.at[:, lanes] for a in outs], *scratch,
        )


def backward_part(gc, gq, vc, kc, rim, sf, taps, gain, dq_o, dk_o, dv_o, gs, qs, ks, vs, table):
    n = gc.shape[0]
    gs[:n] = gc[...]
    gs[n : n + HALO] = rim[:HALO]
    gs[n + HALO :] = jnp.zeros((gs.shape[0] - n - HALO, LANES), BF16)
    toeplitz_into(table, taps[...])
    window = jnp.concatenate([gs[: 2 * LANES], gs[LANES : 3 * LANES]], axis=1)
    res = pick_groups(jnp.dot(table[...], window, preferred_element_type=F32), LANES)
    small = jnp.concatenate([table[g * LANES : g * LANES + HEAD] for g in range(8)], axis=0)
    tail = pick_groups(jnp.dot(small, gs[2 * LANES :], preferred_element_type=F32), HEAD)
    gp = jnp.concatenate([res[:, :LANES], res[:, LANES:]], axis=0) + gain[...] * gs[:n].astype(F32)
    gp_tail = tail + gain[...] * gs[n : n + HEAD].astype(F32)
    qs[:n] = gq[...]
    qs[n:] = rim[HALO + 0 * HEAD : HALO + 1 * HEAD].astype(F32)
    ks[:n] = gp * vc[...]
    ks[n:] = gp_tail * rim[HALO + 1 * HEAD : HALO + 2 * HEAD].astype(F32)
    vs[:n] = gp * kc[...]
    vs[n:] = gp_tail * rim[HALO + 2 * HEAD : HALO + 3 * HEAD].astype(F32)

    def short(scr, member):
        acc = sf[member, 0:1, :] * scr[pl.ds(0, n), :]
        for s in range(1, 7):
            acc = acc + sf[member, s : s + 1, :] * scr[pl.ds(s, n), :]
        return acc.astype(BF16)

    dq_o[...] = short(qs, 0)
    dk_o[...] = short(ks, 1)
    dv_o[...] = short(vs, 2)


def backward(gc, gq, vc, kc, rim, sf, taps, gain, after):
    n, ch = gc.shape
    col = lambda rows: pl.BlockSpec((rows, PARTS * LANES), lambda i: (0, i))
    return pl.pallas_call(
        backward_kernel,
        grid=(ch // LANES // PARTS,),
        in_specs=[
            col(n), col(n), col(n), col(n), col(HALO + 3 * HEAD),
            pl.BlockSpec((3, 7, PARTS * LANES), lambda i: (0, 0, i)),
            pl.BlockSpec((PARTS * 8, 2 * LANES), lambda i: (i, 0)),
            col(1),
        ]
        + any_specs(len(after)),
        out_specs=[col(n)] * 3,
        out_shape=[jax.ShapeDtypeStruct((n, ch), BF16)] * 3,
        scratch_shapes=[
            pltpu.VMEM((4 * LANES, LANES), BF16),
            pltpu.VMEM((n + HEAD, LANES), F32),
            pltpu.VMEM((n + HEAD, LANES), F32),
            pltpu.VMEM((n + HEAD, LANES), F32),
            pltpu.VMEM((8 * LANES, 2 * LANES), BF16),
        ],
        compiler_params=pltpu.CompilerParams(vmem_limit_bytes=VMEM_LIMIT),
        cost_estimate=cost(8),
        name="backward",
    )(gc, gq, vc, kc, rim, sf, taps, gain, *after)


def grad_kernel(n_blocks, last, cols, *refs):
    blocks, w = refs[:n_blocks], refs[n_blocks]
    acc = refs[-1]
    i = pl.program_id(0)
    for k in range(n_blocks):

        @pl.when(i == k)
        def _():
            part = lax.dot_general(
                blocks[k][...], w[...], (((1,), (1,)), ((), ())), preferred_element_type=F32
            )
            if k == 0 and last:
                acc[...] = part + refs[n_blocks + 1][...]
            elif k == 0:
                acc[...] = part
            else:
                acc[...] += part

    if not last:

        @pl.when(i == n_blocks - 1)
        def _():
            refs[-2][...] = acc[...]

        return

    query_conv, carried, value_conv, key_conv = refs[n_blocks + 2 : n_blocks + 6]
    gc_o, gq_o, rim_o = refs[-4:-1]

    @pl.when(i == n_blocks - 1)
    def _():
        grad_carried = (acc[...] * query_conv[...]).astype(BF16)
        gc_o[...] = grad_carried
        gq = acc[...] * carried[...]
        gq_o[...] = gq
        rim_o[:HALO] = grad_carried[:HALO]
        for k, rows in enumerate((gq, value_conv, key_conv)):
            rim_o[HALO + k * HEAD : HALO + (k + 1) * HEAD] = rows[:HEAD].astype(BF16)


def grad_product(cols, blocks, w, rest=(), after=(), us=6.4):
    n = len(blocks)
    rows, width = blocks[0].shape
    ch = w.shape[0]
    whole = lambda r: pl.BlockSpec((r, ch), lambda i, s: (0, 0))
    if rest:
        outs = [
            jax.ShapeDtypeStruct((rows, ch), BF16),
            jax.ShapeDtypeStruct((rows, ch), F32),
            jax.ShapeDtypeStruct((HALO + 3 * HEAD, ch), BF16),
        ]
        rest_specs = [whole(rows)] * 3 + [whole(HEAD)] * 2
    else:
        outs, rest_specs = [jax.ShapeDtypeStruct((rows, ch), F32)], []
    return pl.pallas_call(
        functools.partial(grad_kernel, n, bool(rest)),
        grid_spec=pltpu.PrefetchScalarGridSpec(
            num_scalar_prefetch=1,
            grid=(n,),
            in_specs=[whole(rows)] * n
            + [pl.BlockSpec((ch, width), lambda i, s: (0, s[i]))]
            + rest_specs
            + any_specs(len(after)),
            out_specs=[whole(o.shape[0]) for o in outs],
            scratch_shapes=[pltpu.VMEM((rows, ch), F32)],
        ),
        out_shape=outs,
        compiler_params=pltpu.CompilerParams(vmem_limit_bytes=VMEM_MOST),
        cost_estimate=cost(us),
        name="grad_product",
    )(cols, *blocks, w, *rest, *after)


def project_kernel(n, cols, qg, w, *refs):
    i = pl.program_id(0)
    part = jnp.dot(qg[...], w[...], preferred_element_type=F32)
    for k in range(n):

        @pl.when(i == k)
        def _():
            refs[k - n][...] = part.astype(refs[k - n].dtype)


def project(cols, qg, w, kinds, after=(), us=3.2):
    n = len(kinds)
    rows, ch = qg.shape
    whole = pl.BlockSpec((rows, ch), lambda i, s: (0, 0))
    return pl.pallas_call(
        functools.partial(project_kernel, n),
        grid_spec=pltpu.PrefetchScalarGridSpec(
            num_scalar_prefetch=1,
            grid=(n,),
            in_specs=[whole, pl.BlockSpec((ch, ch), lambda i, s: (0, s[i]))] + any_specs(len(after)),
            out_specs=[whole] * n,
        ),
        out_shape=[jax.ShapeDtypeStruct((rows, ch), kind) for kind in kinds],
        compiler_params=pltpu.CompilerParams(vmem_limit_bytes=VMEM_MOST),
        cost_estimate=cost(us),
        name="project",
    )(cols, qg, w, *after)


def select_kernel(first, width, places, *refs):
    blocks, outs, sems = refs[:8], refs[-5:-1], refs[-1]
    core = places[8]
    for o in range(4):
        for t in range(2):
            for u in range(2):
                start = pl.multiple_of((core if u == 0 else 1 - core) * 512 + first, LANES)
                place = outs[o].at[:, pl.ds((2 * t + u) * width, width)]
                for k in range(8):

                    @pl.when(places[2 * o + t] == k)
                    def _():
                        pltpu.make_async_copy(
                            blocks[k].at[:, pl.ds(start, width)], place, sems.at[4 * o + 2 * t + u]
                        ).start()

    for o in range(4):
        for q in range(4):
            place = outs[o].at[:, pl.ds(q * width, width)]
            pltpu.make_async_copy(blocks[0].at[:, pl.ds(0, width)], place, sems.at[4 * o + q]).wait()


def select(places, blocks, first, width, after=(), us=2.5):
    rows = blocks[0].shape[0]
    return pl.pallas_call(
        functools.partial(select_kernel, first, width),
        in_specs=[pl.BlockSpec(memory_space=pltpu.SMEM)] + any_specs(8 + len(after)),
        out_specs=[pl.BlockSpec(memory_space=pltpu.VMEM)] * 4,
        out_shape=[jax.ShapeDtypeStruct((rows, 4 * width), BF16)] * 4,
        scratch_shapes=[pltpu.SemaphoreType.DMA((16,))],
        compiler_params=pltpu.CompilerParams(vmem_limit_bytes=VMEM_LIMIT),
        cost_estimate=cost(us),
        name="select",
    )(places, *blocks, *after)


def weight_kernel(scale, q0, q1, q2, q3, g0, g1, g2, g3, *refs):
    keep, give = refs[-2:]
    width = g0.shape[1] // 4
    total = jnp.dot(q0[...], g0[...], preferred_element_type=F32)
    total = total + jnp.dot(q1[...], g1[...], preferred_element_type=F32)
    total = total + jnp.dot(q2[...], g2[...], preferred_element_type=F32)
    total = total + jnp.dot(q3[...], g3[...], preferred_element_type=F32)
    total = (total * scale).astype(BF16)
    for t in range(2):
        keep[t] = total[:, 2 * t * width : (2 * t + 1) * width]
        give[t] = total[:, (2 * t + 1) * width : (2 * t + 2) * width]


def weight_sum(left, got, scale, after=()):
    ch, n = left[0].shape
    width = got[0].shape[1] // 4
    tile = 256
    rows = pl.BlockSpec((tile, n), lambda i: (i, 0))
    right = pl.BlockSpec((n, 4 * width), lambda i: (0, 0))
    return pl.pallas_call(
        functools.partial(weight_kernel, scale),
        grid=(ch // tile,),
        in_specs=[rows] * 4 + [right] * 4 + any_specs(len(after)),
        out_specs=[pl.BlockSpec((2, tile, width), lambda i: (0, i, 0))] * 2,
        out_shape=[jax.ShapeDtypeStruct((2, ch, width), BF16)] * 2,
        compiler_params=pltpu.CompilerParams(vmem_limit_bytes=VMEM_LIMIT),
        cost_estimate=cost(0.2),
        name="weight_sum",
    )(*left, *got, *after)


def last_rows_kernel(q, k_before, k, v_before, v, sf, out, ks, vs):
    for scratch, before, tail in ((ks, k_before, k), (vs, v_before, v)):
        scratch[:HEAD] = before[...].astype(F32)
        scratch[HEAD:] = tail[...].astype(F32)
    rows = k.shape[0]
    kc = sf[1, 0:1, :] * ks[HEAD:]
    vc = sf[2, 0:1, :] * vs[HEAD:]
    for s in range(1, 7):
        kc = kc + sf[1, s : s + 1, :] * ks[pl.ds(HEAD - s, rows), :]
        vc = vc + sf[2, s : s + 1, :] * vs[pl.ds(HEAD - s, rows), :]
    out[:HEAD] = q[...]
    out[HEAD : 2 * HEAD] = k[rows - HEAD :]
    out[2 * HEAD : 3 * HEAD] = v[rows - HEAD :]
    out[3 * HEAD :] = (kc * vc).astype(BF16)


def last_rows(q, k, v, sf):
    n, ch = q.shape
    width = 512
    part = lambda rows, i: pl.BlockSpec((rows, width), lambda j: (i, j))
    tail = part(LANES, n // LANES - 1)
    before = part(HEAD, (n - LANES) // HEAD - 1)
    return pl.pallas_call(
        last_rows_kernel,
        grid=(ch // width,),
        in_specs=[part(HEAD, n // HEAD - 1), before, tail, before, tail]
        + [pl.BlockSpec((3, 7, width), lambda j: (0, 0, j))],
        out_specs=part(3 * HEAD + LANES, 0),
        out_shape=jax.ShapeDtypeStruct((3 * HEAD + LANES, ch), BF16),
        scratch_shapes=[pltpu.VMEM((HEAD + LANES, width), F32)] * 2,
        compiler_params=pltpu.CompilerParams(vmem_limit_bytes=VMEM_ALL),
        cost_estimate=cost(1),
        name="last_rows",
    )(q, k, k, v, v, sf)


def wave_kernel(right, left, got, *refs):
    refs[-2][...] = right[...]
    refs[-1][...] = (left[...].astype(F32) + got[...].astype(F32)).astype(BF16)


def wave(right, left, got, after):
    rows, ch = right.shape
    spec = pl.BlockSpec((rows // 2, ch), lambda i: (i, 0))
    return pl.pallas_call(
        wave_kernel,
        grid=(2,),
        in_specs=[spec] * 3 + any_specs(len(after)),
        out_specs=[spec, spec],
        out_shape=[jax.ShapeDtypeStruct((rows, ch), BF16)] * 2,
        compiler_params=pltpu.CompilerParams(vmem_limit_bytes=VMEM_LIMIT),
        cost_estimate=cost(8),
        name="wave",
    )(right, left, got, *after)


def combine_kernel(kept, from_core, *refs):
    refs[-1][...] = (kept[0].astype(F32) + from_core[0].astype(F32)).astype(BF16)


def combine(kept, from_core, after, us):
    _, rows, width = kept.shape
    tile = 256
    second = pl.BlockSpec((1, tile, width), lambda i: (1, i, 0))
    return pl.pallas_call(
        combine_kernel,
        grid=(rows // tile,),
        in_specs=[second, second] + any_specs(len(after)),
        out_specs=pl.BlockSpec((tile, width), lambda i: (i, 0)),
        out_shape=jax.ShapeDtypeStruct((rows, width), BF16),
        compiler_params=pltpu.CompilerParams(vmem_limit_bytes=VMEM_LIMIT),
        cost_estimate=cost(us),
        name="combine",
    )(kept, from_core, *after)


def finish_kernel(kept, from_core, from_yl, *refs):
    before, out = refs[:-1], refs[-1]
    width = from_yl.shape[1]
    total = kept[0].astype(F32) + from_core[0].astype(F32) + from_yl[...].astype(F32)
    if before:
        out[:, :-width] = before[0][...]
        out[:, -width:] = total.astype(BF16)
    else:
        out[...] = total.astype(BF16)


def finish(kept, from_core, from_yl, us, before=()):
    tile = 256
    rows, width = from_yl.shape
    both = pl.BlockSpec((1, tile, width), lambda i: (0, i, 0))
    plain = lambda a: pl.BlockSpec((tile, a.shape[1]), lambda i: (i, 0))
    total = width + sum(a.shape[1] for a in before)
    return pl.pallas_call(
        finish_kernel,
        grid=(rows // tile,),
        in_specs=[both, both, plain(from_yl)] + [plain(a) for a in before],
        out_specs=pl.BlockSpec((tile, total), lambda i: (i, 0)),
        out_shape=jax.ShapeDtypeStruct((rows, total), BF16),
        compiler_params=pltpu.CompilerParams(vmem_limit_bytes=VMEM_LIMIT),
        cost_estimate=cost(us),
        name="finish",
    )(kept, from_core, from_yl, *before)


def on_device(query_in, key_in, value_in, short_filter, long_filter, skip_gain, out_weight, grad_output):
    n, ch = query_in.shape
    ctx, tp = lax.axis_index("ctx"), lax.axis_index("tp")
    z, yl, c = ctx // 4, (ctx // 2) % 2, ctx % 2
    yh, x = tp // 4, tp % 4
    gain = skip_gain.reshape(1, ch)
    w = out_weight

    own = grad_output
    r1, l1 = along_x(own, 1), along_x(own, -1)
    other = across_yh(own)
    halo = next_shard(last_rows(query_in, key_in, value_in, short_filter), 1)
    taps = long_filter.astype(F32).T
    none = jnp.zeros((taps.shape[0], 1), F32)
    pad = jnp.zeros((taps.shape[0], taps.shape[1] - 1), F32)
    taps_fwd = jnp.concatenate([none, taps[:, ::-1], pad], axis=1)
    taps_bwd = jnp.concatenate([taps, none, pad], axis=1)
    query_conv, carried, key_conv, value_conv, gated, gated_t = forward(
        query_in, key_in, value_in, halo, short_filter, toeplitz_table(taps_fwd), gain, [other, r1, l1]
    )

    r2, l2 = along_x(other, 1), along_x(other, -1)
    after_r2, _ = lax.optimization_barrier((r1, r2))
    r3, l3 = along_x(after_r2, 1), along_x(l2, -1)

    left = [gated_t, along_z(gated_t, 1), along_z(gated_t, -1), along_z(gated_t, 2)]

    def block_cols(dys, dxs):
        dy, dx = jnp.array(dys), jnp.array(dxs)
        return (((yh + dy) % YH) * X + (x + dx) % X).astype(jnp.int32)

    near_gg = grad_product(block_cols([0, 0, 1, 1], [3, 1, 3, 1]), [r1, l1, r2, l2], w)

    far_up, far_down = project(
        block_cols([1, 0], [2, 2]), gated, w, [BF16, BF16], after=near_gg
    )

    plane = (z + jnp.array([0, 1, 3, 2])) % Z
    parity = (yl + jnp.array([0, 1])) % 2
    to_x = (2 * (plane % 2))[:, None] + parity[None]
    dy, dx = (plane // 2 + yh) % 2, (to_x - x) % X
    places = jnp.array([0, 2, 6, 1, 3, 5, 7, 4])[dy[:, None] * 4 + dx].reshape(8)
    places = jnp.concatenate([places, c[None]]).astype(jnp.int32)
    blocks = [own, r1, l1, other, r2, l2, r3, l3]
    splits = [(0, 384), (384, 128)]
    first = select(places, blocks, *splits[0], after=[far_up])
    far_up, far_down, _ = lax.optimization_barrier((far_up, far_down, first[0]))
    got_r, got_l = along_x(far_up, 1), along_x(far_down, -1)

    right1, left1 = project(block_cols([1, 1], [1, 3]), gated, w, [F32, BF16], after=[first[0], *left], us=6)
    right0, left0, stay0, stay1 = project(
        block_cols([0, 0, 0, 1], [1, 3, 0, 0]), gated, w, [BF16, BF16, BF16, BF16], after=[left1, got_r, got_l, *left], us=8
    )
    second = select(places, blocks, *splits[1], after=[stay1], us=0.2)
    grad_carried, grad_query_conv, rim = grad_product(
        block_cols([0, 0, 1, 1], [0, 2, 0, 2]), [own, r3, other, l3], w,
        (near_gg[0], query_conv, carried, value_conv, key_conv), after=[second[0]], us=0.2,
    )

    from_r1 = along_x((right1.astype(F32) + got_r.astype(F32)).astype(BF16), 1)
    from_l1 = along_x(left1, -1)
    swap = (stay1.astype(F32) + from_r1.astype(F32) + from_l1.astype(F32)).astype(BF16)
    swapped = across_yh(swap)

    scale = float(n * Z * YL * CORE) ** -0.5

    *second, _ = lax.optimization_barrier((*second, swap))
    rim, _ = lax.optimization_barrier((rim, swap))
    rim = next_shard(rim, -1)

    def over_z(keep, up, down, across):
        return [keep, along_z(up, 1), along_z(down, -1), along_z(across, 2)]

    kept_a, given_a = weight_sum(left, over_z(*first), scale, [grad_carried, swap])
    core_a = across_core(given_a)
    waves = wave(right0, left0, got_l, [kept_a])
    sent_a = combine(kept_a, core_a, [waves[0]], 0.2)
    grad_query, grad_key, grad_value = backward(
        grad_carried, grad_query_conv, value_conv, key_conv, rim,
        short_filter, taps_bwd, gain, [swapped, sent_a],
    )
    beyond, _ = lax.optimization_barrier((second[3], sent_a))
    second = [*second[:3], beyond]
    kept_b, given_b = weight_sum(left, over_z(*second), scale, [grad_query])
    done_a = finish(kept_a, core_a, across_yl(sent_a), 20)
    core_b = across_core(given_b)
    sent_b = combine(kept_b, core_b, [done_a], 0.2)
    weight_grad = finish(kept_b, core_b, across_yl(sent_b), 1, [done_a])

    *waves, _ = lax.optimization_barrier((*waves, grad_query))
    from_r0, from_l0 = along_x(waves[0], 1), along_x(waves[1], -1)
    output = stay0.astype(F32) + from_r0.astype(F32) + from_l0.astype(F32) + swapped.astype(F32)
    output = output.astype(BF16)
    return output, grad_query, grad_key, grad_value, weight_grad


def solution(mesh):
    return jax.shard_map(
        on_device,
        mesh=mesh,
        in_specs=(
            P("ctx", "tp"),
            P("ctx", "tp"),
            P("ctx", "tp"),
            P(None, None, "tp"),
            P(None, "tp"),
            P("tp"),
            P("tp", None),
            P("ctx", "tp"),
        ),
        out_specs=(P("ctx", "tp"), P("ctx", "tp"), P("ctx", "tp"), P("ctx", "tp"), P("tp", "ctx")),
        check_vma=False,
    )
```

```python
import functools

import jax
import jax.numpy as jnp
from jax import lax
from jax.experimental import pallas as pl
from jax.experimental.pallas import tpu as pltpu
from jax.sharding import PartitionSpec as P

Z, YL, CORE, YH, X = 4, 2, 2, 2, 4
F32, BF16 = jnp.float32, jnp.bfloat16
HALO = 144
HEAD = 16
LANES = 128
PARTS = 4
VMEM_LIMIT = 16 * 1024 * 1024
VMEM_ALL = 60 * 1024 * 1024
VMEM_MOST = 48 * 1024 * 1024


def cost(us):
    return pl.CostEstimate(flops=int(us * 4.6e9), bytes_accessed=2**16, transcendentals=0)


def ctx_pairs(move):
    pairs = []
    for i in range(Z * YL * CORE):
        z, yl, c = move(i // 4, (i // 2) % 2, i % 2)
        pairs.append((i, (z % Z) * 4 + (yl % YL) * 2 + c % CORE))
    return pairs


def tp_pairs(move):
    pairs = []
    for j in range(YH * X):
        yh, x = move(j // 4, j % 4)
        pairs.append((j, (yh % YH) * 4 + x % X))
    return pairs


def along_x(a, d):
    return lax.ppermute(a, "tp", tp_pairs(lambda yh, x: (yh, x + d)))


def across_yh(a):
    return lax.ppermute(a, "tp", tp_pairs(lambda yh, x: (yh + 1, x)))


def along_z(a, d):
    return lax.ppermute(a, "ctx", ctx_pairs(lambda z, yl, c: (z + d, yl, c)))


def across_core(a):
    return lax.ppermute(a, "ctx", ctx_pairs(lambda z, yl, c: (z, yl, c + 1)))


def next_shard(a, d):
    n = Z * YL * CORE
    return lax.ppermute(a, "ctx", [(i, i + d) for i in range(n) if 0 <= i + d < n])


def across_yl(a):
    return lax.ppermute(a, "ctx", ctx_pairs(lambda z, yl, c: (z, yl + 1, c)))


def any_specs(n):
    return [pl.BlockSpec(memory_space=pl.ANY)] * n


def toeplitz_into(table, rows):
    for g in range(8):
        wide = jnp.broadcast_to(rows[g : g + 1, :], (LANES, 2 * LANES))
        table[g * LANES : (g + 1) * LANES, :] = pltpu.roll(
            wide, 0, 1, stride=1, stride_axis=0
        ).astype(BF16)


def pick_groups(res, rows):
    lane_group = (lax.broadcasted_iota(jnp.int32, (rows, res.shape[1]), 1) % LANES) // 16
    out = res[:rows]
    for g in range(1, 8):
        out = jnp.where(lane_group == g, res[g * rows : (g + 1) * rows], out)
    return out


def table_kernel(taps, out):
    toeplitz_into(out, taps[...])


def toeplitz_table(taps):
    groups, window = taps.shape
    return pl.pallas_call(
        table_kernel,
        grid=(groups // 8,),
        in_specs=[pl.BlockSpec((8, window), lambda i: (i, 0))],
        out_specs=pl.BlockSpec((8 * LANES, window), lambda i: (i, 0)),
        out_shape=jax.ShapeDtypeStruct((groups * LANES, window), BF16),
        compiler_params=pltpu.CompilerParams(vmem_limit_bytes=VMEM_LIMIT),
        cost_estimate=cost(6),
        name="toeplitz_table",
    )(taps)


def forward_kernel(q, k, v, halo, sf, table, gain, *refs):
    outs, scratch = refs[-9:-3], refs[-3:]
    for part in range(PARTS):
        lanes, rows = pl.ds(part * LANES, LANES), pl.ds(part * 8 * LANES, 8 * LANES)
        forward_part(
            *[a.at[:, lanes] for a in (q, k, v, halo)], sf.at[:, :, lanes], table.at[rows], gain.at[:, lanes],
            *[a.at[:, lanes] for a in outs[:5]], outs[5].at[lanes], *scratch,
        )


def forward_part(q, k, v, halo, sf, table, gain, qc_o, ca_o, kc_o, vc_o, qg_o, qgt_o, qs, ks, vs):
    n = q.shape[0]
    qs[:HEAD] = halo[:HEAD].astype(F32)
    qs[HEAD:] = q[...].astype(F32)
    ks[:HEAD] = halo[HEAD : 2 * HEAD].astype(F32)
    ks[HEAD:] = k[...].astype(F32)
    vs[:HEAD] = halo[2 * HEAD : 3 * HEAD].astype(F32)
    vs[HEAD:] = v[...].astype(F32)

    def short(scr, member, first, rows):
        acc = sf[member, 0:1, :] * scr[pl.ds(first, rows), :]
        for s in range(1, 7):
            acc = acc + sf[member, s : s + 1, :] * scr[pl.ds(first - s, rows), :]
        return acc

    qc = short(qs, 0, HEAD, n)
    kc = short(ks, 1, HEAD, n)
    vc = short(vs, 2, HEAD, n)
    kv = jnp.concatenate([halo[3 * HEAD :], (kc * vc).astype(BF16)], axis=0)
    window = jnp.concatenate([kv[: 2 * LANES], kv[LANES:]], axis=1)
    res = pick_groups(jnp.dot(table[...], window, preferred_element_type=F32), LANES)
    carried = jnp.concatenate([res[:, :LANES], res[:, LANES:]], axis=0)
    carried = carried + gain[...] * kv[LANES:].astype(F32)
    qc_o[...] = qc
    ca_o[...] = carried
    kc_o[...] = kc
    vc_o[...] = vc
    gated = qc * carried
    qg_o[...] = gated.astype(BF16)
    qgt_o[...] = gated.T.astype(BF16)


def forward(q, k, v, halo, sf, table, gain, after):
    n, ch = q.shape
    col = lambda rows: pl.BlockSpec((rows, PARTS * LANES), lambda i: (0, i))
    return pl.pallas_call(
        forward_kernel,
        grid=(ch // LANES // PARTS,),
        in_specs=[
            col(n), col(n), col(n), col(3 * HEAD + LANES),
            pl.BlockSpec((3, 7, PARTS * LANES), lambda i: (0, 0, i)),
            pl.BlockSpec((PARTS * 8 * LANES, 2 * LANES), lambda i: (i, 0)),
            col(1),
        ]
        + [pl.BlockSpec(memory_space=pl.ANY)] * len(after),
        out_specs=[col(n)] * 5 + [pl.BlockSpec((PARTS * LANES, n), lambda i: (i, 0))],
        out_shape=[jax.ShapeDtypeStruct((n, ch), F32)] * 4
        + [jax.ShapeDtypeStruct((n, ch), BF16), jax.ShapeDtypeStruct((ch, n), BF16)],
        scratch_shapes=[
            pltpu.VMEM((HEAD + n, LANES), F32),
            pltpu.VMEM((HEAD + n, LANES), F32),
            pltpu.VMEM((HEAD + n, LANES), F32),
        ],
        compiler_params=pltpu.CompilerParams(vmem_limit_bytes=VMEM_ALL),
        cost_estimate=cost(8),
        name="forward",
    )(q, k, v, halo, sf, table, gain, *after)


def backward_kernel(gc, gq, vc, kc, rim, sf, taps, gain, *refs):
    outs, scratch = refs[-8:-5], refs[-5:]
    for part in range(PARTS):
        lanes, rows = pl.ds(part * LANES, LANES), pl.ds(part * 8, 8)
        backward_part(
            *[a.at[:, lanes] for a in (gc, gq, vc, kc, rim)], sf.at[:, :, lanes], taps.at[rows],
            gain.at[:, lanes], *[a.at[:, lanes] for a in outs], *scratch,
        )


def backward_part(gc, gq, vc, kc, rim, sf, taps, gain, dq_o, dk_o, dv_o, gs, qs, ks, vs, table):
    n = gc.shape[0]
    gs[:n] = gc[...]
    gs[n : n + HALO] = rim[:HALO]
    gs[n + HALO :] = jnp.zeros((gs.shape[0] - n - HALO, LANES), BF16)
    toeplitz_into(table, taps[...])
    window = jnp.concatenate([gs[: 2 * LANES], gs[LANES : 3 * LANES]], axis=1)
    res = pick_groups(jnp.dot(table[...], window, preferred_element_type=F32), LANES)
    small = jnp.concatenate([table[g * LANES : g * LANES + HEAD] for g in range(8)], axis=0)
    tail = pick_groups(jnp.dot(small, gs[2 * LANES :], preferred_element_type=F32), HEAD)
    gp = jnp.concatenate([res[:, :LANES], res[:, LANES:]], axis=0) + gain[...] * gs[:n].astype(F32)
    gp_tail = tail + gain[...] * gs[n : n + HEAD].astype(F32)
    qs[:n] = gq[...]
    qs[n:] = rim[HALO + 0 * HEAD : HALO + 1 * HEAD].astype(F32)
    ks[:n] = gp * vc[...]
    ks[n:] = gp_tail * rim[HALO + 1 * HEAD : HALO + 2 * HEAD].astype(F32)
    vs[:n] = gp * kc[...]
    vs[n:] = gp_tail * rim[HALO + 2 * HEAD : HALO + 3 * HEAD].astype(F32)

    def short(scr, member):
        acc = sf[member, 0:1, :] * scr[pl.ds(0, n), :]
        for s in range(1, 7):
            acc = acc + sf[member, s : s + 1, :] * scr[pl.ds(s, n), :]
        return acc.astype(BF16)

    dq_o[...] = short(qs, 0)
    dk_o[...] = short(ks, 1)
    dv_o[...] = short(vs, 2)


def backward(gc, gq, vc, kc, rim, sf, taps, gain, after):
    n, ch = gc.shape
    col = lambda rows: pl.BlockSpec((rows, PARTS * LANES), lambda i: (0, i))
    return pl.pallas_call(
        backward_kernel,
        grid=(ch // LANES // PARTS,),
        in_specs=[
            col(n), col(n), col(n), col(n), col(HALO + 3 * HEAD),
            pl.BlockSpec((3, 7, PARTS * LANES), lambda i: (0, 0, i)),
            pl.BlockSpec((PARTS * 8, 2 * LANES), lambda i: (i, 0)),
            col(1),
        ]
        + any_specs(len(after)),
        out_specs=[col(n)] * 3,
        out_shape=[jax.ShapeDtypeStruct((n, ch), BF16)] * 3,
        scratch_shapes=[
            pltpu.VMEM((4 * LANES, LANES), BF16),
            pltpu.VMEM((n + HEAD, LANES), F32),
            pltpu.VMEM((n + HEAD, LANES), F32),
            pltpu.VMEM((n + HEAD, LANES), F32),
            pltpu.VMEM((8 * LANES, 2 * LANES), BF16),
        ],
        compiler_params=pltpu.CompilerParams(vmem_limit_bytes=VMEM_LIMIT),
        cost_estimate=cost(8),
        name="backward",
    )(gc, gq, vc, kc, rim, sf, taps, gain, *after)


def grad_kernel(n_blocks, last, cols, *refs):
    blocks, w = refs[:n_blocks], refs[n_blocks]
    acc = refs[-1]
    i = pl.program_id(0)
    for k in range(n_blocks):

        @pl.when(i == k)
        def _():
            part = lax.dot_general(
                blocks[k][...], w[...], (((1,), (1,)), ((), ())), preferred_element_type=F32
            )
            if k == 0 and last:
                acc[...] = part + refs[n_blocks + 1][...]
            elif k == 0:
                acc[...] = part
            else:
                acc[...] += part

    if not last:

        @pl.when(i == n_blocks - 1)
        def _():
            refs[-2][...] = acc[...]

        return

    query_conv, carried, value_conv, key_conv = refs[n_blocks + 2 : n_blocks + 6]
    gc_o, gq_o, rim_o = refs[-4:-1]

    @pl.when(i == n_blocks - 1)
    def _():
        grad_carried = (acc[...] * query_conv[...]).astype(BF16)
        gc_o[...] = grad_carried
        gq = acc[...] * carried[...]
        gq_o[...] = gq
        rim_o[:HALO] = grad_carried[:HALO]
        for k, rows in enumerate((gq, value_conv, key_conv)):
            rim_o[HALO + k * HEAD : HALO + (k + 1) * HEAD] = rows[:HEAD].astype(BF16)


def grad_product(cols, blocks, w, rest=(), after=(), us=6.4):
    n = len(blocks)
    rows, width = blocks[0].shape
    ch = w.shape[0]
    whole = lambda r: pl.BlockSpec((r, ch), lambda i, s: (0, 0))
    if rest:
        outs = [
            jax.ShapeDtypeStruct((rows, ch), BF16),
            jax.ShapeDtypeStruct((rows, ch), F32),
            jax.ShapeDtypeStruct((HALO + 3 * HEAD, ch), BF16),
        ]
        rest_specs = [whole(rows)] * 3 + [whole(HEAD)] * 2
    else:
        outs, rest_specs = [jax.ShapeDtypeStruct((rows, ch), F32)], []
    return pl.pallas_call(
        functools.partial(grad_kernel, n, bool(rest)),
        grid_spec=pltpu.PrefetchScalarGridSpec(
            num_scalar_prefetch=1,
            grid=(n,),
            in_specs=[whole(rows)] * n
            + [pl.BlockSpec((ch, width), lambda i, s: (0, s[i]))]
            + rest_specs
            + any_specs(len(after)),
            out_specs=[whole(o.shape[0]) for o in outs],
            scratch_shapes=[pltpu.VMEM((rows, ch), F32)],
        ),
        out_shape=outs,
        compiler_params=pltpu.CompilerParams(vmem_limit_bytes=VMEM_MOST),
        cost_estimate=cost(us),
        name="grad_product",
    )(cols, *blocks, w, *rest, *after)


def project_kernel(n, cols, qg, w, *refs):
    i = pl.program_id(0)
    part = jnp.dot(qg[...], w[...], preferred_element_type=F32)
    for k in range(n):

        @pl.when(i == k)
        def _():
            refs[k - n][...] = part.astype(refs[k - n].dtype)


def project(cols, qg, w, kinds, after=(), us=3.2):
    n = len(kinds)
    rows, ch = qg.shape
    whole = pl.BlockSpec((rows, ch), lambda i, s: (0, 0))
    return pl.pallas_call(
        functools.partial(project_kernel, n),
        grid_spec=pltpu.PrefetchScalarGridSpec(
            num_scalar_prefetch=1,
            grid=(n,),
            in_specs=[whole, pl.BlockSpec((ch, ch), lambda i, s: (0, s[i]))] + any_specs(len(after)),
            out_specs=[whole] * n,
        ),
        out_shape=[jax.ShapeDtypeStruct((rows, ch), kind) for kind in kinds],
        compiler_params=pltpu.CompilerParams(vmem_limit_bytes=VMEM_MOST),
        cost_estimate=cost(us),
        name="project",
    )(cols, qg, w, *after)


def select_kernel(first, width, places, *refs):
    blocks, outs, sems = refs[:8], refs[-5:-1], refs[-1]
    core = places[8]
    for o in range(4):
        for t in range(2):
            for u in range(2):
                start = pl.multiple_of((core if u == 0 else 1 - core) * 512 + first, LANES)
                place = outs[o].at[:, pl.ds((2 * t + u) * width, width)]
                for k in range(8):

                    @pl.when(places[2 * o + t] == k)
                    def _():
                        pltpu.make_async_copy(
                            blocks[k].at[:, pl.ds(start, width)], place, sems.at[4 * o + 2 * t + u]
                        ).start()

    for o in range(4):
        for q in range(4):
            place = outs[o].at[:, pl.ds(q * width, width)]
            pltpu.make_async_copy(blocks[0].at[:, pl.ds(0, width)], place, sems.at[4 * o + q]).wait()


def select(places, blocks, first, width, after=(), us=2.5):
    rows = blocks[0].shape[0]
    return pl.pallas_call(
        functools.partial(select_kernel, first, width),
        in_specs=[pl.BlockSpec(memory_space=pltpu.SMEM)] + any_specs(8 + len(after)),
        out_specs=[pl.BlockSpec(memory_space=pltpu.VMEM)] * 4,
        out_shape=[jax.ShapeDtypeStruct((rows, 4 * width), BF16)] * 4,
        scratch_shapes=[pltpu.SemaphoreType.DMA((16,))],
        compiler_params=pltpu.CompilerParams(vmem_limit_bytes=VMEM_LIMIT),
        cost_estimate=cost(us),
        name="select",
    )(places, *blocks, *after)


def weight_kernel(scale, q0, q1, q2, q3, g0, g1, g2, g3, *refs):
    keep, give = refs[-2:]
    width = g0.shape[1] // 4
    total = jnp.dot(q0[...], g0[...], preferred_element_type=F32)
    total = total + jnp.dot(q1[...], g1[...], preferred_element_type=F32)
    total = total + jnp.dot(q2[...], g2[...], preferred_element_type=F32)
    total = total + jnp.dot(q3[...], g3[...], preferred_element_type=F32)
    total = (total * scale).astype(BF16)
    for t in range(2):
        keep[t] = total[:, 2 * t * width : (2 * t + 1) * width]
        give[t] = total[:, (2 * t + 1) * width : (2 * t + 2) * width]


def weight_sum(left, got, scale, after=()):
    ch, n = left[0].shape
    width = got[0].shape[1] // 4
    tile = 256
    rows = pl.BlockSpec((tile, n), lambda i: (i, 0))
    right = pl.BlockSpec((n, 4 * width), lambda i: (0, 0))
    return pl.pallas_call(
        functools.partial(weight_kernel, scale),
        grid=(ch // tile,),
        in_specs=[rows] * 4 + [right] * 4 + any_specs(len(after)),
        out_specs=[pl.BlockSpec((2, tile, width), lambda i: (0, i, 0))] * 2,
        out_shape=[jax.ShapeDtypeStruct((2, ch, width), BF16)] * 2,
        compiler_params=pltpu.CompilerParams(vmem_limit_bytes=VMEM_LIMIT),
        cost_estimate=cost(0.2),
        name="weight_sum",
    )(*left, *got, *after)


def last_rows_kernel(q, k_before, k, v_before, v, sf, out, ks, vs):
    for scratch, before, tail in ((ks, k_before, k), (vs, v_before, v)):
        scratch[:HEAD] = before[...].astype(F32)
        scratch[HEAD:] = tail[...].astype(F32)
    rows = k.shape[0]
    kc = sf[1, 0:1, :] * ks[HEAD:]
    vc = sf[2, 0:1, :] * vs[HEAD:]
    for s in range(1, 7):
        kc = kc + sf[1, s : s + 1, :] * ks[pl.ds(HEAD - s, rows), :]
        vc = vc + sf[2, s : s + 1, :] * vs[pl.ds(HEAD - s, rows), :]
    out[:HEAD] = q[...]
    out[HEAD : 2 * HEAD] = k[rows - HEAD :]
    out[2 * HEAD : 3 * HEAD] = v[rows - HEAD :]
    out[3 * HEAD :] = (kc * vc).astype(BF16)


def last_rows(q, k, v, sf):
    n, ch = q.shape
    width = 512
    part = lambda rows, i: pl.BlockSpec((rows, width), lambda j: (i, j))
    tail = part(LANES, n // LANES - 1)
    before = part(HEAD, (n - LANES) // HEAD - 1)
    return pl.pallas_call(
        last_rows_kernel,
        grid=(ch // width,),
        in_specs=[part(HEAD, n // HEAD - 1), before, tail, before, tail]
        + [pl.BlockSpec((3, 7, width), lambda j: (0, 0, j))],
        out_specs=part(3 * HEAD + LANES, 0),
        out_shape=jax.ShapeDtypeStruct((3 * HEAD + LANES, ch), BF16),
        scratch_shapes=[pltpu.VMEM((HEAD + LANES, width), F32)] * 2,
        compiler_params=pltpu.CompilerParams(vmem_limit_bytes=VMEM_ALL),
        cost_estimate=cost(1),
        name="last_rows",
    )(q, k, k, v, v, sf)


def wave_kernel(right, left, got, *refs):
    refs[-2][...] = right[...]
    refs[-1][...] = (left[...].astype(F32) + got[...].astype(F32)).astype(BF16)


def wave(right, left, got, after):
    rows, ch = right.shape
    spec = pl.BlockSpec((rows // 2, ch), lambda i: (i, 0))
    return pl.pallas_call(
        wave_kernel,
        grid=(2,),
        in_specs=[spec] * 3 + any_specs(len(after)),
        out_specs=[spec, spec],
        out_shape=[jax.ShapeDtypeStruct((rows, ch), BF16)] * 2,
        compiler_params=pltpu.CompilerParams(vmem_limit_bytes=VMEM_LIMIT),
        cost_estimate=cost(8),
        name="wave",
    )(right, left, got, *after)


def combine_kernel(kept, from_core, *refs):
    refs[-1][...] = (kept[0].astype(F32) + from_core[0].astype(F32)).astype(BF16)


def combine(kept, from_core, after, us):
    _, rows, width = kept.shape
    tile = 256
    second = pl.BlockSpec((1, tile, width), lambda i: (1, i, 0))
    return pl.pallas_call(
        combine_kernel,
        grid=(rows // tile,),
        in_specs=[second, second] + any_specs(len(after)),
        out_specs=pl.BlockSpec((tile, width), lambda i: (i, 0)),
        out_shape=jax.ShapeDtypeStruct((rows, width), BF16),
        compiler_params=pltpu.CompilerParams(vmem_limit_bytes=VMEM_LIMIT),
        cost_estimate=cost(us),
        name="combine",
    )(kept, from_core, *after)


def finish_kernel(kept, from_core, from_yl, *refs):
    before, out = refs[:-1], refs[-1]
    width = from_yl.shape[1]
    total = kept[0].astype(F32) + from_core[0].astype(F32) + from_yl[...].astype(F32)
    if before:
        out[:, :-width] = before[0][...]
        out[:, -width:] = total.astype(BF16)
    else:
        out[...] = total.astype(BF16)


def finish(kept, from_core, from_yl, us, before=()):
    tile = 256
    rows, width = from_yl.shape
    both = pl.BlockSpec((1, tile, width), lambda i: (0, i, 0))
    plain = lambda a: pl.BlockSpec((tile, a.shape[1]), lambda i: (i, 0))
    total = width + sum(a.shape[1] for a in before)
    return pl.pallas_call(
        finish_kernel,
        grid=(rows // tile,),
        in_specs=[both, both, plain(from_yl)] + [plain(a) for a in before],
        out_specs=pl.BlockSpec((tile, total), lambda i: (i, 0)),
        out_shape=jax.ShapeDtypeStruct((rows, total), BF16),
        compiler_params=pltpu.CompilerParams(vmem_limit_bytes=VMEM_LIMIT),
        cost_estimate=cost(us),
        name="finish",
    )(kept, from_core, from_yl, *before)


def on_device(query_in, key_in, value_in, short_filter, long_filter, skip_gain, out_weight, grad_output):
    n, ch = query_in.shape
    ctx, tp = lax.axis_index("ctx"), lax.axis_index("tp")
    z, yl, c = ctx // 4, (ctx // 2) % 2, ctx % 2
    yh, x = tp // 4, tp % 4
    gain = skip_gain.reshape(1, ch)
    w = out_weight

    own = grad_output
    r1, l1 = along_x(own, 1), along_x(own, -1)
    other = across_yh(own)
    halo = next_shard(last_rows(query_in, key_in, value_in, short_filter), 1)
    taps = long_filter.astype(F32).T
    none = jnp.zeros((taps.shape[0], 1), F32)
    pad = jnp.zeros((taps.shape[0], taps.shape[1] - 1), F32)
    taps_fwd = jnp.concatenate([none, taps[:, ::-1], pad], axis=1)
    taps_bwd = jnp.concatenate([taps, none, pad], axis=1)
    query_conv, carried, key_conv, value_conv, gated, gated_t = forward(
        query_in, key_in, value_in, halo, short_filter, toeplitz_table(taps_fwd), gain, [other, r1, l1]
    )

    r2, l2 = along_x(other, 1), along_x(other, -1)
    after_r2, _ = lax.optimization_barrier((r1, r2))
    r3, l3 = along_x(after_r2, 1), along_x(l2, -1)

    left = [gated_t, along_z(gated_t, 1), along_z(gated_t, -1), along_z(gated_t, 2)]

    def block_cols(dys, dxs):
        dy, dx = jnp.array(dys), jnp.array(dxs)
        return (((yh + dy) % YH) * X + (x + dx) % X).astype(jnp.int32)

    near_gg = grad_product(block_cols([0, 0, 1, 1], [3, 1, 3, 1]), [r1, l1, r2, l2], w)

    far_up, far_down = project(
        block_cols([1, 0], [2, 2]), gated, w, [BF16, BF16], after=near_gg
    )

    plane = (z + jnp.array([0, 1, 3, 2])) % Z
    parity = (yl + jnp.array([0, 1])) % 2
    to_x = (2 * (plane % 2))[:, None] + parity[None]
    dy, dx = (plane // 2 + yh) % 2, (to_x - x) % X
    places = jnp.array([0, 2, 6, 1, 3, 5, 7, 4])[dy[:, None] * 4 + dx].reshape(8)
    places = jnp.concatenate([places, c[None]]).astype(jnp.int32)
    blocks = [own, r1, l1, other, r2, l2, r3, l3]
    splits = [(0, 384), (384, 128)]
    first = select(places, blocks, *splits[0], after=[far_up])
    far_up, far_down, _ = lax.optimization_barrier((far_up, far_down, first[0]))
    got_r, got_l = along_x(far_up, 1), along_x(far_down, -1)

    right1, left1 = project(block_cols([1, 1], [1, 3]), gated, w, [F32, BF16], after=[first[0], *left], us=6)
    right0, left0, stay0, stay1 = project(
        block_cols([0, 0, 0, 1], [1, 3, 0, 0]), gated, w, [BF16, BF16, BF16, BF16], after=[left1, got_r, got_l, *left], us=8
    )
    second = select(places, blocks, *splits[1], after=[stay1], us=0.2)
    grad_carried, grad_query_conv, rim = grad_product(
        block_cols([0, 0, 1, 1], [0, 2, 0, 2]), [own, r3, other, l3], w,
        (near_gg[0], query_conv, carried, value_conv, key_conv), after=[second[0]], us=0.2,
    )

    from_r1 = along_x((right1.astype(F32) + got_r.astype(F32)).astype(BF16), 1)
    from_l1 = along_x(left1, -1)
    swap = (stay1.astype(F32) + from_r1.astype(F32) + from_l1.astype(F32)).astype(BF16)
    swapped = across_yh(swap)

    scale = float(n * Z * YL * CORE) ** -0.5

    *second, _ = lax.optimization_barrier((*second, swap))
    rim, _ = lax.optimization_barrier((rim, swap))
    rim = next_shard(rim, -1)

    def over_z(keep, up, down, across):
        return [keep, along_z(up, 1), along_z(down, -1), along_z(across, 2)]

    kept_a, given_a = weight_sum(left, over_z(*first), scale, [grad_carried, swap])
    core_a = across_core(given_a)
    waves = wave(right0, left0, got_l, [kept_a])
    sent_a = combine(kept_a, core_a, [waves[0]], 0.2)
    grad_query, grad_key, grad_value = backward(
        grad_carried, grad_query_conv, value_conv, key_conv, rim,
        short_filter, taps_bwd, gain, [swapped, sent_a],
    )
    beyond, _ = lax.optimization_barrier((second[3], sent_a))
    second = [*second[:3], beyond]
    kept_b, given_b = weight_sum(left, over_z(*second), scale, [grad_query])
    done_a = finish(kept_a, core_a, across_yl(sent_a), 20)
    core_b = across_core(given_b)
    sent_b = combine(kept_b, core_b, [done_a], 0.2)
    weight_grad = finish(kept_b, core_b, across_yl(sent_b), 1, [done_a])

    *waves, _ = lax.optimization_barrier((*waves, grad_query))
    from_r0, from_l0 = along_x(waves[0], 1), along_x(waves[1], -1)
    output = stay0.astype(F32) + from_r0.astype(F32) + from_l0.astype(F32) + swapped.astype(F32)
    output = output.astype(BF16)
    return output, grad_query, grad_key, grad_value, weight_grad


def solution(mesh):
    return jax.shard_map(
        on_device,
        mesh=mesh,
        in_specs=(
            P("ctx", "tp"),
            P("ctx", "tp"),
            P("ctx", "tp"),
            P(None, None, "tp"),
            P(None, "tp"),
            P("tp"),
            P("tp", None),
            P("ctx", "tp"),
        ),
        out_specs=(P("ctx", "tp"), P("ctx", "tp"), P("ctx", "tp"), P("ctx", "tp"), P("tp", "ctx")),
        check_vma=False,
    )
```
